256 devices in a mesh: tok: 4 (over z_hi, core), col: 64 (over y, x, z_lo).
Axes of the slice: x: 4, y: 4, z: 8 (z_hi: 2, z_lo: 4; z = z_hi * 4 + z_lo), core: 2. Of those that a mesh axis runs over, the one named last changes fastest.
Arguments:
- acts_t: bfloat16 [4096, 2048], P('col', 'tok'), may hold values from -6 to 6
- grads_t: bfloat16 [14336, 2048], P('col', 'tok'), may hold values from -6 to 6
- basis_a: bfloat16 [4096, 4096], P('col'), may hold values from -0.09375 to 0.09375
- basis_g: bfloat16 [14336, 14336], P('col'), may hold values from -0.046875 to 0.046875
Outputs:
- scaling: float32 [14336, 4096], P('col', 'tok')
The draws below stay inside these ranges and needn't reach their ends.
All inputs are finite; a program needn't handle non-finite values.
Results may differ from the reference program's by a relative error of at most 0.0003.
Values may be sent and summed in bfloat16 or wider, within the bound.
A program may use at most 128 MiB of HBM per device.

```python
import jax
import jax.numpy as jnp
from jax import lax

D = 4096
FF = 14336
TOK_DEV = 512
TOKENS = 2048
N_TOK = 4


def steps_of(own_key, shape, shards, least, largest):
    def one(position, blocks):
        draws = jax.random.uniform(jax.random.fold_in(jax.random.fold_in(own_key, 6), position), (blocks,), jnp.float32, least / len(shards), largest / len(shards))
        return jnp.repeat(jnp.exp(draws), shape[position] // blocks).reshape((-1,) + (1,) * (len(shape) - position - 1))

    loudness = one(*shards[0])
    for cut in shards[1:]:
        loudness = loudness * one(*cut)
    return loudness


def normal_values(own_key, shape, width, bound, cuts=(), kind=jnp.bfloat16):
    result = jax.random.normal(own_key, shape, jnp.float32) * width
    if len(cuts) > 0:
        result = steps_of(own_key, shape, cuts, -0.22, 0.18) * result
    return jnp.clip(result, min=-bound, max=bound).astype(kind)


def setup_inputs(seed: int = 0) -> dict:
    streams_of = jax.random.split(jax.random.key(seed), 5)
    acts_t = normal_values(streams_of[0], (D, TOKENS), 1.0, 6.0, ((0, 64), (1, 4)))
    grads_t = normal_values(streams_of[1], (FF, TOKENS), 1.0, 6.0, ((0, 64), (1, 4)))
    basis_a = normal_values(streams_of[2], (D, D), D ** -0.5, 0.09375, ((0, 64),))
    basis_g = normal_values(streams_of[3], (FF, FF), FF ** -0.5, 0.046875, ((0, 64),))
    return {"acts_t": acts_t, "grads_t": grads_t, "basis_a": basis_a, "basis_g": basis_g}


def reference(acts_t, grads_t, basis_a, basis_g):
    proj_a = jnp.dot(basis_a, acts_t, preferred_element_type=jnp.float32)
    sq_a = (proj_a * proj_a).astype(jnp.bfloat16)
    proj_g = jnp.dot(basis_g, grads_t, preferred_element_type=jnp.float32)
    sq_g = (proj_g * proj_g).astype(jnp.bfloat16)
    total = jnp.zeros((sq_g.shape[0], sq_a.shape[0]), jnp.float32)
    for block in range(N_TOK):
        block_g = sq_g[:, block * TOK_DEV:(block + 1) * TOK_DEV]
        block_a = sq_a[:, block * TOK_DEV:(block + 1) * TOK_DEV]
        partial_value = lax.dot_general(block_g, block_a, (((1,), (1,)), ((), ())), preferred_element_type=jnp.float32)
        total = total + partial_value
    return total / jnp.float32(TOKENS)
```

```python
import jax
import jax.numpy as jnp
from jax import lax
from jax.experimental import pallas as pl
from jax.experimental.pallas import tpu as pltpu
from jax.sharding import PartitionSpec as P

MESH = pl.DeviceIdType.MESH
BF16 = jnp.bfloat16
F32 = jnp.float32
NX, NY, NZ, NT = 4, 4, 4, 4


class Sems:
    def __init__(self, send, recv):
        self.send, self.recv, self.used = send, recv, 0

    def take(self):
        i = self.used
        self.used += 1
        return self.send.at[i], self.recv.at[i]


N_COPIES = 104
N_LOCAL = 12


def kernel(acts, grads, basis_a, basis_g, out, xa, ba, pa, ra, sa, sq, xg, bg, acc, ps, pr, sg,
           send_sem, recv_sem, local_sem):
    tok = lax.axis_index("tok")
    col = lax.axis_index("col")
    zl = lax.rem(col, 4)
    x = lax.rem(lax.div(col, 4), 4)
    y = lax.div(col, 16)
    c = lax.rem(tok, 2)
    da, fa = acts.shape[0], basis_a.shape[1] // NY
    dg = grads.shape[0]
    half = dg // 2
    fx = NZ * dg
    fy = NX * fx
    cols = acts.shape[1]
    quarter = cols // NY

    def up(v, d):
        return lax.rem(v + d, 4)

    def dn(v, d):
        return lax.rem(v + 4 - d, 4)

    def dev(tok=tok, y=y, x=x, zl=zl):
        return (tok, (y * 4 + x) * 4 + zl)

    sib = tok + 1 - 2 * c
    far = up(tok, 2)

    barrier = pltpu.get_barrier_semaphore()
    partners = [dev(tok=up(tok, dt), zl=up(zl, dz)) for dt in range(4) for dz in range(4) if dt or dz]
    partners += [dev(x=up(x, d)) for d in (1, 2, 3)] + [dev(y=up(y, d)) for d in (1, 2, 3)]
    for p in partners:
        pl.semaphore_signal(barrier, inc=1, device_id=p, device_id_type=MESH)
    pl.semaphore_wait(barrier, len(partners))

    sems = Sems(send_sem, recv_sem)
    sent = []

    class Copy:
        def __init__(self, tag, landing):
            self.tag, self.landing, self.sems = tag, landing, sems.take()

        def start(self, src, dst, to):
            s, r = self.sems
            cp = pltpu.make_async_remote_copy(src_ref=src, dst_ref=dst, send_sem=s, recv_sem=r,
                                              device_id=to, device_id_type=MESH)
            cp.start()
            sent.append(cp)

        def arrived(self):
            s, r = self.sems
            pltpu.make_async_remote_copy(src_ref=self.landing, dst_ref=self.landing, send_sem=s, recv_sem=r,
                                         device_id=dev(), device_id_type=MESH).wait_recv()

    n_local = [0]

    def local(src, dst):
        cp = pltpu.make_async_copy(src, dst, local_sem.at[n_local[0]])
        n_local[0] += 1
        cp.start()
        return cp

    def xa_at(xs, zs):
        return xa.at[pl.ds(pl.multiple_of(xs * (NZ * da) + zs * da, da), da), :]

    def ba_at(ys):
        return ba.at[pl.ds(pl.multiple_of(ys * da, da), da), :]

    def ba_cols(ys):
        return basis_a.at[:, pl.ds(pl.multiple_of(ys * fa, fa), fa)]

    def xg_at(ys, zs):
        return xg.at[ys, pl.ds(pl.multiple_of(zs * dg, 32), dg), :]

    def bg_at(h, ys, xs):
        return bg.at[h, ys, pl.ds(pl.multiple_of(xs * half, 16), half), :]

    def bg_cols(h, ys, xs):
        return basis_g.at[h * half:(h + 1) * half, pl.ds(pl.multiple_of(ys * fy + xs * fx, 128), fx)]

    def sq_block(t, xs, zs, q):
        return sq.at[t, pl.ds(pl.multiple_of((xs * NZ + zs) * da, da), da), pl.ds(pl.multiple_of(q * quarter, quarter), quarter)]

    def sq_chunk(xs, q):
        return sq.at[:, pl.ds(pl.multiple_of(xs * (NZ * da), NZ * da), NZ * da), pl.ds(pl.multiple_of(q * quarter, quarter), quarter)]

    three = (1, 3, 2)

    a_z = {d: Copy("a_z", xa_at(x, dn(zl, d))) for d in three}
    a_x = {(j, d): Copy("a_x", xa_at(dn(x, d), dn(zl, j))) for j in range(4) for d in three}
    b_a = {d: Copy("b_a", ba_at(dn(y, d))) for d in three}
    g_z = {d: Copy("g_z", xg_at(y, dn(zl, d))) for d in three}
    g_y = {(j, d): Copy("g_y", xg_at(dn(y, d), dn(zl, j))) for j in range(4) for d in (1, 3)}
    g_f = {j: Copy("g_f", xg_at(up(y, 2), dn(zl, j))) for j in range(4)}
    mine = [up(y, 3 * c), up(y, 1 + c)]
    theirs = [up(y, 3 * (1 - c)), up(y, 2 - c)]
    b_x = {(h, k, d): Copy("b_x", bg_at(h, mine[k], dn(x, d))) for h in range(2) for k in range(2) for d in three}
    b_s = {(h, k, d): Copy("b_s", bg_at(h, theirs[k], dn(x, d))) for h in range(2) for k in range(2) for d in three}

    def send_grads_z(d):
        g_z[d].start(grads, xg_at(y, zl), dev(zl=up(zl, d)))

    def send_basis(h, k, d):
        b_x[h, k, d].start(bg_cols(h, mine[k], up(x, d)), bg_at(h, mine[k], x), dev(x=up(x, d)))

    def share_basis(h, k):
        for d in three:
            b_x[h, k, d].arrived()
            b_s[h, k, d].start(bg_at(h, mine[k], dn(x, d)), bg_at(h, mine[k], dn(x, d)), dev(tok=sib))

    def spread_grads(j):
        g_z[j].arrived()
        for d in (1, 3):
            g_y[j, d].start(xg_at(y, dn(zl, j)), xg_at(y, dn(zl, j)), dev(y=up(y, d)))

    def forward_grads(j):
        d = 1 if j < 2 else 3
        g_y[j, d].arrived()
        g_f[j].start(xg_at(dn(y, d), dn(zl, j)), xg_at(dn(y, d), dn(zl, j)), dev(y=up(y, d)))

    for d in three:
        a_z[d].start(acts, xa_at(x, zl), dev(zl=up(zl, d)))
    for d in three:
        a_x[0, d].start(acts, xa_at(x, zl), dev(x=up(x, d)))
    for d in three:
        b_a[d].start(ba_cols(up(y, d)), ba_at(y), dev(y=up(y, d)))
    send_grads_z(1)
    for d in (1, 3):
        g_y[0, d].start(grads, xg_at(y, zl), dev(y=up(y, d)))
    for d in (1, 3):
        send_basis(0, 0, d)
    a_own = local(acts, xa_at(x, zl))
    ba_own = local(ba_cols(y), ba_at(y))
    g_own = local(grads, xg_at(y, zl))
    bg_own = [local(bg_cols(h, ys, x), bg_at(h, ys, x)) for h in range(2) for ys in mine + theirs]

    for j in three:
        a_z[j].arrived()
        for d in three:
            a_x[j, d].start(xa_at(x, dn(zl, j)), xa_at(x, dn(zl, j)), dev(x=up(x, d)))
    send_grads_z(3)
    send_grads_z(2)
    send_basis(0, 0, 2)
    for d in three:
        send_basis(0, 1, d)
    spread_grads(1)
    forward_grads(0)

    a_own.wait()
    ba_own.wait()
    for d in three:
        b_a[d].arrived()
    for key in a_x:
        a_x[key].arrived()
    for ys in range(NY):
        pa[ys] = jnp.dot(ba[...], xa[:, ys * quarter:(ys + 1) * quarter], preferred_element_type=F32)
    p_a = {d: Copy("p_a", ra.at[d - 1]) for d in three}
    for d in three:
        p_a[d].start(pa.at[up(y, d)], ra.at[d - 1], dev(y=up(y, d)))
    spread_grads(3)
    forward_grads(1)
    share_basis(0, 0)
    for d in three:
        p_a[d].arrived()
    total_a = pa[y] + ra[0] + ra[1] + ra[2]
    sa[...] = (total_a * total_a).astype(BF16)

    s_z = {(dt, dz): Copy("s_z", sq_block(dn(tok, dt), x, dn(zl, dz), y)) for dt in range(4) for dz in range(4) if dt or dz}
    for dt, dz in s_z:
        t = up(tok, dt)
        s_z[dt, dz].start(sa.at[pl.ds(pl.multiple_of(t * da, da), da), :], sq_block(tok, x, zl, y),
                          dev(tok=t, zl=up(zl, dz)))
    s_own = local(sa.at[pl.ds(pl.multiple_of(tok * da, da), da), :], sq_block(tok, x, zl, y))
    s_x = {d: Copy("s_x", sq_chunk(dn(x, d), y)) for d in three}
    s_y = {(j, d): Copy("s_y", sq_chunk(dn(x, j), dn(y, d))) for j in range(4) for d in (1, 3)}
    s_f = {j: Copy("s_f", sq_chunk(dn(x, j), up(y, 2))) for j in range(4)}

    def spread_sq(j):
        for d in (1, 3):
            s_y[j, d].start(sq_chunk(dn(x, j), y), sq_chunk(dn(x, j), y), dev(y=up(y, d)))

    def forward_sq(j):
        d = 1 if j < 2 else 3
        s_y[j, d].arrived()
        s_f[j].start(sq_chunk(dn(x, j), dn(y, d)), sq_chunk(dn(x, j), dn(y, d)), dev(y=up(y, d)))

    spread_grads(2)
    for d in three:
        send_basis(1, 0, d)
    s_own.wait()
    for key in s_z:
        s_z[key].arrived()
    for d in three:
        s_x[d].start(sq_chunk(x, y), sq_chunk(x, y), dev(x=up(x, d)))
    spread_sq(0)
    share_basis(0, 1)
    for d in three:
        send_basis(1, 1, d)
    forward_grads(3)
    forward_grads(2)

    g_own.wait()
    for cp in bg_own:
        cp.wait()

    def basis_there(h, k):
        for d in three:
            b_s[h, k, d].arrived()

    def add_range(h, ys, first=False):
        part = jnp.dot(bg[h, ys], xg[ys], preferred_element_type=F32)
        acc[h] = part if first else acc[h] + part

    p_g = {(h, d): Copy("p_g", pr.at[h, d - 1]) for h in range(2) for d in three}

    def exchange_products(h):
        ps[h] = acc[h].astype(BF16)
        for d in (2, 1, 3):
            xs = up(x, d)
            p_g[h, d].start(ps.at[h, pl.ds(pl.multiple_of(xs * half, 16), half), :], pr.at[h, d - 1], dev(x=xs))

    def sg_at(t, h):
        return sg.at[t, h * half:(h + 1) * half, :]

    t_far = [Copy("t_far", sg_at(far, h)) for h in range(2)]
    t_sib = [Copy("t_sib", sg_at(sib, h)) for h in range(2)]
    t_both = [Copy("t_both", sg_at(up(sib, 2), h)) for h in range(2)]

    def square_products(h):
        for d in three:
            p_g[h, d].arrived()
        own = acc[h, pl.ds(pl.multiple_of(x * half, 8), half), :]
        total = own + pr[h, 0].astype(F32) + pr[h, 1].astype(F32) + pr[h, 2].astype(F32)
        sg[tok, h * half:(h + 1) * half, :] = (total * total).astype(BF16)
        t_far[h].start(sg_at(tok, h), sg_at(tok, h), dev(tok=far))
        t_sib[h].start(sg_at(tok, h), sg_at(tok, h), dev(tok=sib))

    def share_tokens(h):
        t_far[h].arrived()
        t_both[h].start(sg_at(far, h), sg_at(far, h), dev(tok=sib))

    basis_there(0, 0)
    add_range(0, y, True)
    basis_there(0, 1)
    for d in (1, 3):
        for j in range(4):
            if (j < 2) != (d == 1):
                g_y[j, d].arrived()
        add_range(0, dn(y, d))
    for j in range(4):
        g_f[j].arrived()
    add_range(0, up(y, 2))
    exchange_products(0)
    share_basis(1, 0)
    forward_sq(0)
    for j in three:
        s_x[j].arrived()
        spread_sq(j)
    basis_there(1, 0)
    add_range(1, y, True)
    add_range(1, dn(y, 1))
    square_products(0)
    forward_sq(1)
    share_basis(1, 1)
    basis_there(1, 1)
    add_range(1, up(y, 1))
    add_range(1, up(y, 2))
    exchange_products(1)
    share_tokens(0)
    forward_sq(3)
    square_products(1)
    forward_sq(2)
    for j in range(4):
        for d in (1, 3):
            if (j < 2) != (d == 1):
                s_y[j, d].arrived()
        s_f[j].arrived()

    tile = 256
    scale = 1.0 / (cols * NT)

    def add_tokens(t, first, final):
        for n in range(0, out.shape[1], tile):
            part = lax.dot_general(sg[t], sq[t, n:n + tile, :], (((1,), (1,)), ((), ())), preferred_element_type=F32)
            value = part if first else out[:, n:n + tile] + part
            out[:, n:n + tile] = value * scale if final else value

    add_tokens(tok, True, False)
    for h in range(2):
        t_sib[h].arrived()
    add_tokens(sib, False, False)
    share_tokens(1)
    add_tokens(far, False, False)
    for h in range(2):
        t_both[h].arrived()
    add_tokens(up(sib, 2), False, True)

    for cp in sent:
        cp.wait_send()


def body(acts_t, grads_t, basis_a, basis_g):
    da, cols = acts_t.shape
    dg = grads_t.shape[0]
    fa = basis_a.shape[1] // NY
    rows_a, quarter = NY * da, cols // NY
    fx, half = NZ * dg, dg // 2
    anywhere = pl.BlockSpec(memory_space=pl.ANY)
    n_out = basis_a.shape[1] // NT
    return pl.pallas_call(
        kernel,
        out_shape=jax.ShapeDtypeStruct((dg, n_out), F32),
        in_specs=[anywhere] * 4,
        out_specs=pl.BlockSpec(memory_space=pltpu.VMEM),
        scratch_shapes=[
            pltpu.VMEM((fa, cols), BF16),
            pltpu.VMEM((rows_a, fa), BF16),
            pltpu.VMEM((NY, rows_a, quarter), F32),
            pltpu.VMEM((NY - 1, rows_a, quarter), F32),
            pltpu.VMEM((rows_a, quarter), BF16),
            pltpu.VMEM((NT, n_out, cols), BF16),
            pltpu.VMEM((NY, fx, cols), BF16),
            pltpu.VMEM((2, NY, NX * half, fx), BF16),
            pltpu.VMEM((2, NX * half, cols), F32),
            pltpu.VMEM((2, NX * half, cols), BF16),
            pltpu.VMEM((2, NX - 1, half, cols), BF16),
            pltpu.VMEM((NT, dg, cols), BF16),
            pltpu.SemaphoreType.DMA((N_COPIES,)),
            pltpu.SemaphoreType.DMA((N_COPIES,)),
            pltpu.SemaphoreType.DMA((N_LOCAL,)),
        ],
        compiler_params=pltpu.CompilerParams(
            collective_id=0, has_side_effects=True, vmem_limit_bytes=60 * 2**20
        ),
    )(acts_t, grads_t, basis_a, basis_g)


def solution(mesh):
    return jax.shard_map(
        body,
        mesh=mesh,
        in_specs=(P("col", "tok"), P("col", "tok"), P("col", None), P("col", None)),
        out_specs=P("col", "tok"),
        check_vma=False,
    )
```

```python
import jax
import jax.numpy as jnp
from jax import lax
from jax.experimental import pallas as pl
from jax.experimental.pallas import tpu as pltpu
from jax.sharding import PartitionSpec as P

MESH = pl.DeviceIdType.MESH
BF16 = jnp.bfloat16
F32 = jnp.float32
NX, NY, NZ, NT = 4, 4, 4, 4


class Sems:
    def __init__(self, send, recv):
        self.send, self.recv, self.used = send, recv, 0

    def take(self):
        i = self.used
        self.used += 1
        return self.send.at[i], self.recv.at[i]


N_COPIES = 128
N_LOCAL = 12

THREE = (1, 3, 2)
SIDES = (1, 3)


def way(j):
    return 1 if j < 2 else 3


SCHEDULE = (
    ("bx", 0, 0, 1), ("bx", 0, 0, 3), ("af", 0), ("gz", 2), ("as", 1), ("as", 3), ("as", 2), ("ax", 1), ("ax", 2),
    ("ax", 3), ("bs", 0, 0, 3), ("bs", 0, 0, 1), ("gf", 0), ("bx", 0, 1, 3), ("bx", 0, 1, 1), ("gz", 1), ("af", 2),
    ("af", 3), ("af", 1), ("gs", 2), ("bx", 0, 1, 2), ("pa",), ("bs", 0, 1, 1), ("gf", 2), ("gs", 1),
    ("bs", 0, 1, 3), ("gz", 3), ("bx", 0, 0, 2), ("bs", 0, 1, 2), ("bx", 1, 0, 1), ("bx", 1, 0, 3), ("bs", 0, 0, 2),
    ("bx", 1, 1, 2), ("sa",), ("bs", 1, 0, 3), ("bs", 1, 0, 1), ("gs", 3), ("cg", 0, 0), ("gf", 1), ("bx", 1, 1, 1),
    ("bx", 1, 1, 3), ("bs", 1, 1, 2), ("bx", 1, 0, 2), ("sx",), ("bs", 1, 1, 1), ("bs", 1, 1, 3), ("gf", 3),
    ("uf", 0), ("cg", 0, 1), ("cg", 0, 2), ("us", 2), ("sf", 0), ("ss", 3), ("sxf", 1), ("bs", 1, 0, 2), ("uf", 2),
    ("sxf", 0), ("ss", 1), ("cg", 0, 3), ("cg", 1, 0), ("cg", 1, 1), ("ss", 2), ("cg", 1, 2), ("cg", 1, 3),
    ("sf", 3), ("sq", 0), ("sq", 1), ("us", 1), ("us", 3), ("sf", 1), ("sf", 2), ("tb", 0), ("uf", 1), ("uf", 3),
    ("tb", 1), ("fin", 0), ("fin", 1), ("fin", 2), ("fin", 3),
)


SPLIT = 3


def kernel(acts, grads, basis_a, basis_g, out, xa, ba, pa, ra, sa, sq, xg, bg, acc, ps, pr, sg,
           send_sem, recv_sem, local_sem):
    tok = lax.axis_index("tok")
    col = lax.axis_index("col")
    zl = lax.rem(col, 4)
    x = lax.rem(lax.div(col, 4), 4)
    y = lax.div(col, 16)
    c = lax.rem(tok, 2)
    da, fa = acts.shape[0], basis_a.shape[1] // NY
    dg = grads.shape[0]
    half = dg // 2
    fx = NZ * dg
    fy = NX * fx
    cols = acts.shape[1]
    quarter = cols // NY

    def up(v, d):
        return lax.rem(v + d, 4)

    def dn(v, d):
        return lax.rem(v + 4 - d, 4)

    def dev(tok=tok, y=y, x=x, zl=zl):
        return (tok, (y * 4 + x) * 4 + zl)

    sib = tok + 1 - 2 * c
    far = up(tok, 2)

    barrier = pltpu.get_barrier_semaphore()
    partners = [dev(tok=up(tok, dt), zl=up(zl, dz)) for dt in range(4) for dz in range(4) if dt or dz]
    partners += [dev(x=up(x, d)) for d in (1, 2, 3)] + [dev(y=up(y, d)) for d in (1, 2, 3)]
    for p in partners:
        pl.semaphore_signal(barrier, inc=1, device_id=p, device_id_type=MESH)
    pl.semaphore_wait(barrier, len(partners))

    sems = Sems(send_sem, recv_sem)
    sent = []

    class Copy:
        def __init__(self, tag, landing):
            self.tag, self.landing, self.sems, self.here = tag, landing, sems.take(), False

        def start(self, src, dst, to):
            s, r = self.sems
            cp = pltpu.make_async_remote_copy(src_ref=src, dst_ref=dst, send_sem=s, recv_sem=r,
                                              device_id=to, device_id_type=MESH)
            cp.start()
            sent.append(cp)

        def arrived(self):
            if self.here:
                return
            self.here = True
            s, r = self.sems
            pltpu.make_async_remote_copy(src_ref=self.landing, dst_ref=self.landing, send_sem=s, recv_sem=r,
                                         device_id=dev(), device_id_type=MESH).wait_recv()

    n_local = [0]

    def local(src, dst):
        cp = pltpu.make_async_copy(src, dst, local_sem.at[n_local[0]])
        n_local[0] += 1
        cp.start()
        return cp

    def xa_at(xs, zs):
        return xa.at[pl.ds(pl.multiple_of(xs * (NZ * da) + zs * da, da), da), :]

    def ba_at(ys, core):
        return ba.at[pl.ds(pl.multiple_of(ys * da + core * (da // 2), da // 2), da // 2), :]

    def ba_cols(ys):
        return pl.ds(pl.multiple_of(ys * fa, fa), fa)

    def xg_at(ys, zs):
        return xg.at[ys, pl.ds(pl.multiple_of(zs * dg, 32), dg), :]

    def bg_at(h, ys, xs):
        return bg.at[h, ys, pl.ds(pl.multiple_of(xs * half, 16), half), :]

    def bg_cols(h, ys, xs):
        return basis_g.at[h * half:(h + 1) * half, pl.ds(pl.multiple_of(ys * fy + xs * fx, 128), fx)]

    def lanes(q):
        return pl.ds(pl.multiple_of(q * quarter, quarter), quarter)

    def sq_block(t, xs, zs, q):
        return sq.at[t, pl.ds(pl.multiple_of((xs * NZ + zs) * da, da), da), lanes(q)]

    def sq_chunk(xs, q, first=0, rows=NZ * da):
        return sq.at[0:SPLIT, pl.ds(pl.multiple_of(xs * (NZ * da) + first, 128), rows), lanes(q)]

    def sq_rest(xs, q):
        return sq.at[SPLIT:NT, pl.ds(pl.multiple_of(xs * (NZ * da), NZ * da), NZ * da), lanes(q)]

    a_z = {d: Copy("a_z", xa_at(x, dn(zl, d))) for d in THREE}
    a_x = {(j, d): Copy("a_x", xa_at(dn(x, d), dn(zl, j))) for j in range(4) for d in SIDES}
    a_f = {j: Copy("a_f", xa_at(up(x, 2), dn(zl, j))) for j in range(4)}
    b_a = {d: Copy("b_a", ba_at(dn(y, d), c)) for d in THREE}
    a_s = {d: Copy("a_s", ba_at(dn(y, d), 1 - c)) for d in THREE}
    p_a = {d: Copy("p_a", ra.at[d - 1]) for d in THREE}
    g_z = {d: Copy("g_z", xg_at(y, dn(zl, d))) for d in THREE}
    g_y = {(j, d): Copy("g_y", xg_at(dn(y, d), dn(zl, j))) for j in range(4) for d in SIDES}
    g_f = {j: Copy("g_f", xg_at(up(y, 2), dn(zl, j))) for j in range(4)}
    mine = [up(y, 3 * c), up(y, 1 + c)]
    theirs = [up(y, 3 * (1 - c)), up(y, 2 - c)]
    pieces = [(h, k, d) for h in range(2) for k in range(2) for d in THREE]
    b_x = {(h, k, d): Copy("b_x", bg_at(h, mine[k], dn(x, d))) for h, k, d in pieces}
    b_s = {(h, k, d): Copy("b_s", bg_at(h, theirs[k], dn(x, d))) for h, k, d in pieces}
    p_g = {(h, d): Copy("p_g", pr.at[h, d - 1]) for h in range(2) for d in THREE}
    turns = [(dt, dz) for dt in range(4) for dz in range(4) if dt or dz]
    s_z = {(dt, dz): Copy("s_z", sq_block(dn(tok, dt), x, dn(zl, dz), y)) for dt, dz in turns}
    s_x = {d: Copy("s_x", sq_chunk(dn(x, d), y)) for d in SIDES}
    s_xf = [Copy("s_xf", sq_chunk(up(x, 2), y, 128 * i, 128)) for i in range(2)]
    s_y = {(j, d): Copy("s_y", sq_chunk(dn(x, j), dn(y, d))) for j in range(4) for d in SIDES}
    s_f = {j: Copy("s_f", sq_chunk(dn(x, j), up(y, 2))) for j in range(4)}
    u_y = {d: Copy("u_y", sq_rest(x, dn(y, d))) for d in THREE}
    u_x = {(j, d): Copy("u_x", sq_rest(dn(x, d), dn(y, j))) for j in range(4) for d in SIDES}
    u_f = {j: Copy("u_f", sq_rest(up(x, 2), dn(y, j))) for j in range(4)}

    def sg_at(t, h):
        return sg.at[t, h * half:(h + 1) * half, :]

    t_far = [Copy("t_far", sg_at(far, h)) for h in range(2)]
    t_sib = [Copy("t_sib", sg_at(sib, h)) for h in range(2)]
    t_both = [Copy("t_both", sg_at(up(sib, 2), h)) for h in range(2)]

    def all_of(*groups):
        for group in groups:
            for copy in group.values() if isinstance(group, dict) else group:
                copy.arrived()

    for d in THREE:
        a_z[d].start(acts, xa_at(x, zl), dev(zl=up(zl, d)))
    for d in SIDES:
        a_x[0, d].start(acts, xa_at(x, zl), dev(x=up(x, d)))
    for d in THREE:
        b_a[d].start(basis_a.at[pl.ds(pl.multiple_of(c * (da // 2), da // 2), da // 2), ba_cols(up(y, d))], ba_at(y, c),
                     dev(y=up(y, d)))
    for d in SIDES:
        g_y[0, d].start(grads, xg_at(y, zl), dev(y=up(y, d)))
    own_a = [local(acts, xa_at(x, zl)), local(basis_a.at[:, ba_cols(y)], ba.at[pl.ds(pl.multiple_of(y * da, da), da), :])]
    own_g = [local(grads, xg_at(y, zl))]
    own_g += [local(bg_cols(h, ys, x), bg_at(h, ys, x)) for h in range(2) for ys in mine + theirs]
    own_s = []

    def ax(j):
        a_z[j].arrived()
        for d in SIDES:
            a_x[j, d].start(xa_at(x, dn(zl, j)), xa_at(x, dn(zl, j)), dev(x=up(x, d)))

    def af(j):
        d = way(j)
        a_x[j, d].arrived()
        a_f[j].start(xa_at(dn(x, d), dn(zl, j)), xa_at(dn(x, d), dn(zl, j)), dev(x=up(x, d)))

    def share_a(d):
        b_a[d].arrived()
        a_s[d].start(ba_at(dn(y, d), c), ba_at(dn(y, d), c), dev(tok=sib))

    def project_a():
        for cp in own_a:
            cp.wait()
        all_of(a_x, a_f, b_a, a_s)
        for ys in range(NY):
            pa[ys] = jnp.dot(ba[...], xa[:, ys * quarter:(ys + 1) * quarter], preferred_element_type=F32)
        for d in THREE:
            p_a[d].start(pa.at[up(y, d)], ra.at[d - 1], dev(y=up(y, d)))

    def square_a():
        all_of(p_a)
        total = pa[y] + ra[0] + ra[1] + ra[2]
        sa[...] = (total * total).astype(BF16)
        for dt, dz in turns:
            t = up(tok, dt)
            s_z[dt, dz].start(sa.at[pl.ds(pl.multiple_of(t * da, da), da), :], sq_block(tok, x, zl, y),
                              dev(tok=t, zl=up(zl, dz)))
        own_s.append(local(sa.at[pl.ds(pl.multiple_of(tok * da, da), da), :], sq_block(tok, x, zl, y)))

    def spread(j):
        for d in SIDES:
            s_y[j, d].start(sq_chunk(dn(x, j), y), sq_chunk(dn(x, j), y), dev(y=up(y, d)))

    def spread_rest(j):
        for d in SIDES:
            u_x[j, d].start(sq_rest(x, dn(y, j)), sq_rest(x, dn(y, j)), dev(x=up(x, d)))

    def sx():
        own_s[0].wait()
        all_of(s_z)
        for d in SIDES:
            s_x[d].start(sq_chunk(x, y), sq_chunk(x, y), dev(x=up(x, d)))
        spread(0)
        for d in THREE:
            u_y[d].start(sq_rest(x, y), sq_rest(x, y), dev(y=up(y, d)))
        spread_rest(0)

    def sxf(i):
        d = SIDES[i]
        s_x[d].arrived()
        part = sq_chunk(dn(x, d), y, 128 * i, 128)
        s_xf[i].start(part, part, dev(x=up(x, d)))

    def ss(j):
        all_of(s_xf if j == 2 else [s_x[j]])
        spread(j)

    def sf(j):
        d = way(j)
        s_y[j, d].arrived()
        s_f[j].start(sq_chunk(dn(x, j), dn(y, d)), sq_chunk(dn(x, j), dn(y, d)), dev(y=up(y, d)))

    def us(j):
        u_y[j].arrived()
        spread_rest(j)

    def uf(j):
        d = way(j)
        u_x[j, d].arrived()
        u_f[j].start(sq_rest(dn(x, d), dn(y, j)), sq_rest(dn(x, d), dn(y, j)), dev(x=up(x, d)))

    def gz(d):
        g_z[d].start(grads, xg_at(y, zl), dev(zl=up(zl, d)))

    def gs(j):
        g_z[j].arrived()
        for d in SIDES:
            g_y[j, d].start(xg_at(y, dn(zl, j)), xg_at(y, dn(zl, j)), dev(y=up(y, d)))

    def gf(j):
        d = way(j)
        g_y[j, d].arrived()
        g_f[j].start(xg_at(dn(y, d), dn(zl, j)), xg_at(dn(y, d), dn(zl, j)), dev(y=up(y, d)))

    def bx(h, k, d):
        b_x[h, k, d].start(bg_cols(h, mine[k], up(x, d)), bg_at(h, mine[k], x), dev(x=up(x, d)))

    def bs(h, k, d):
        b_x[h, k, d].arrived()
        b_s[h, k, d].start(bg_at(h, mine[k], dn(x, d)), bg_at(h, mine[k], dn(x, d)), dev(tok=sib))

    def cg(h, i):
        while own_g:
            own_g.pop().wait()
        for d in THREE:
            all_of([b_x[h, i // 2, d], b_s[h, i // 2, d]])
        if i == 0:
            all_of(g_z)
        elif i == 3:
            all_of(g_f)
        else:
            all_of([g_y[j, SIDES[i - 1]] for j in range(4)])
        ys = (y, dn(y, 1), up(y, 1), up(y, 2))[i]
        part = jnp.dot(bg[h, ys], xg[ys], preferred_element_type=F32)
        acc[h] = part if i == 0 else acc[h] + part
        if i == 3:
            ps[h] = acc[h].astype(BF16)
            for d in (2, 1, 3):
                xs = up(x, d)
                p_g[h, d].start(ps.at[h, pl.ds(pl.multiple_of(xs * half, 16), half), :], pr.at[h, d - 1], dev(x=xs))

    def square_g(h):
        all_of([p_g[h, d] for d in THREE])
        own = acc[h, pl.ds(pl.multiple_of(x * half, 8), half), :]
        total = own + pr[h, 0].astype(F32) + pr[h, 1].astype(F32) + pr[h, 2].astype(F32)
        sg[tok, h * half:(h + 1) * half, :] = (total * total).astype(BF16)
        t_far[h].start(sg_at(tok, h), sg_at(tok, h), dev(tok=far))
        t_sib[h].start(sg_at(tok, h), sg_at(tok, h), dev(tok=sib))

    def tb(h):
        t_far[h].arrived()
        t_both[h].start(sg_at(far, h), sg_at(far, h), dev(tok=sib))

    tile = 256
    scale = 1.0 / (cols * NT)

    def fin(i):
        all_of(*((s_x, s_xf, s_y, s_f, u_y, u_x, u_f), (t_sib,), (t_far,), (t_both,))[i])
        t = (tok, sib, far, up(sib, 2))[i]
        for n in range(0, out.shape[1], tile):
            part = lax.dot_general(sg[t], sq[t, n:n + tile, :], (((1,), (1,)), ((), ())), preferred_element_type=F32)
            value = part if i == 0 else out[:, n:n + tile] + part
            out[:, n:n + tile] = value * scale if i == 3 else value

    steps = {"ax": ax, "af": af, "as": share_a, "pa": project_a, "sa": square_a, "sx": sx, "sxf": sxf, "ss": ss, "sf": sf,
             "us": us, "uf": uf, "gz": gz, "gs": gs, "gf": gf, "bx": bx, "bs": bs, "cg": cg, "sq": square_g, "tb": tb,
             "fin": fin}
    for name, *where in SCHEDULE:
        steps[name](*where)

    for cp in sent:
        cp.wait_send()


def body(acts_t, grads_t, basis_a, basis_g):
    da, cols = acts_t.shape
    dg = grads_t.shape[0]
    fa = basis_a.shape[1] // NY
    rows_a, quarter = NY * da, cols // NY
    fx, half = NZ * dg, dg // 2
    anywhere = pl.BlockSpec(memory_space=pl.ANY)
    n_out = basis_a.shape[1] // NT
    return pl.pallas_call(
        kernel,
        out_shape=jax.ShapeDtypeStruct((dg, n_out), F32),
        in_specs=[anywhere] * 4,
        out_specs=pl.BlockSpec(memory_space=pltpu.VMEM),
        scratch_shapes=[
            pltpu.VMEM((fa, cols), BF16),
            pltpu.VMEM((rows_a, fa), BF16),
            pltpu.VMEM((NY, rows_a, quarter), F32),
            pltpu.VMEM((NY - 1, rows_a, quarter), F32),
            pltpu.VMEM((rows_a, quarter), BF16),
            pltpu.VMEM((NT, n_out, cols), BF16),
            pltpu.VMEM((NY, fx, cols), BF16),
            pltpu.VMEM((2, NY, NX * half, fx), BF16),
            pltpu.VMEM((2, NX * half, cols), F32),
            pltpu.VMEM((2, NX * half, cols), BF16),
            pltpu.VMEM((2, NX - 1, half, cols), BF16),
            pltpu.VMEM((NT, dg, cols), BF16),
            pltpu.SemaphoreType.DMA((N_COPIES,)),
            pltpu.SemaphoreType.DMA((N_COPIES,)),
            pltpu.SemaphoreType.DMA((N_LOCAL,)),
        ],
        compiler_params=pltpu.CompilerParams(
            collective_id=0, has_side_effects=True, vmem_limit_bytes=60 * 2**20
        ),
    )(acts_t, grads_t, basis_a, basis_g)


def solution(mesh):
    return jax.shard_map(
        body,
        mesh=mesh,
        in_specs=(P("col", "tok"), P("col", "tok"), P("col", None), P("col", None)),
        out_specs=P("col", "tok"),
        check_vma=False,
    )
```

```python
import jax
import jax.numpy as jnp
from jax import lax
from jax.experimental import pallas as pl
from jax.experimental.pallas import tpu as pltpu
from jax.sharding import PartitionSpec as P

MESH = pl.DeviceIdType.MESH
BF16 = jnp.bfloat16
F32 = jnp.float32
NX, NY, NZ, NT = 4, 4, 4, 4


class Sems:
    def __init__(self, send, recv):
        self.send, self.recv, self.used = send, recv, 0

    def take(self):
        i = self.used
        self.used += 1
        return self.send.at[i], self.recv.at[i]


N_COPIES = 144
N_LOCAL = 24

THREE = (1, 3, 2)
SIDES = (1, 3)


def way(j):
    return 1 if j < 2 else 3


SCHEDULE = (
    ("bx", 0, 0, 2), ("ax", 1), ("gz", 2), ("ax", 3), ("gf", 0), ("ax", 2), ("af", 0), ("af", 3), ("af", 1),
    ("as", 3), ("af", 2), ("vz", 0), ("gs", 2), ("as", 2), ("bx", 0, 0, 1), ("gz", 1), ("bx", 0, 0, 3),
    ("bx", 1, 0, 1), ("bs", 0, 0, 2), ("as", 1), ("pa",), ("bx", 1, 0, 3), ("gf", 2), ("gz", 3), ("bx", 0, 1, 1),
    ("bx", 0, 1, 3), ("gs", 1), ("bs", 0, 0, 1), ("bx", 1, 1, 2), ("sa",), ("gs", 3), ("bx", 0, 1, 2),
    ("bs", 0, 0, 3), ("bs", 0, 1, 3), ("sx",), ("bs", 0, 1, 1), ("vz", 3), ("vz", 1), ("bs", 0, 1, 2), ("gf", 3),
    ("gf", 1), ("bx", 1, 0, 2), ("cg", 0, 0), ("vz", 2), ("sxf", 1), ("sxf", 0), ("bs", 1, 1, 2), ("bx", 1, 1, 3),
    ("bs", 1, 0, 3), ("bs", 1, 0, 1), ("cg", 0, 1), ("ss", 3), ("bx", 1, 1, 1), ("cg", 0, 2), ("cg", 0, 3),
    ("bs", 1, 0, 2), ("ss", 2), ("bs", 1, 1, 1), ("ss", 1), ("cg", 1, 0), ("sf", 3), ("cg", 1, 1), ("bs", 1, 1, 3),
    ("cg", 1, 2), ("us", 2), ("sf", 0), ("us", 1), ("cg", 1, 3), ("us", 3), ("sq", 0), ("sf", 2), ("sf", 1),
    ("uf", 1), ("uf", 2), ("sq", 1), ("uf", 3), ("uf", 0), ("tb", 0), ("fin", 0), ("tb", 1), ("fin", 1), ("fin", 2),
    ("fin", 3),
)


SPLIT = 3
PARTS = (160, 64)
FLIP = 32


def kernel(acts, grads, basis_a, basis_g, out, xa, ba, pa, ra, sa, sq, xg, bg, acc, ps, pr, sg,
           send_sem, recv_sem, local_sem):
    tok = lax.axis_index("tok")
    col = lax.axis_index("col")
    zl = lax.rem(col, 4)
    x = lax.rem(lax.div(col, 4), 4)
    y = lax.div(col, 16)
    c = lax.rem(tok, 2)
    da, fa = acts.shape[0], basis_a.shape[1] // NY
    dg = grads.shape[0]
    at = [sum(PARTS[:h]) for h in range(len(PARTS))]
    flip = FLIP
    fx = NZ * dg
    fy = NX * fx
    cols = acts.shape[1]
    quarter = cols // NY

    def up(v, d):
        return lax.rem(v + d, 4)

    def dn(v, d):
        return lax.rem(v + 4 - d, 4)

    def dev(tok=tok, y=y, x=x, zl=zl):
        return (tok, (y * 4 + x) * 4 + zl)

    sib = tok + 1 - 2 * c
    far = up(tok, 2)

    barrier = pltpu.get_barrier_semaphore()
    partners = [dev(tok=up(tok, dt), zl=up(zl, dz)) for dt in range(4) for dz in range(4) if dt or dz]
    partners += [dev(x=up(x, d)) for d in (1, 2, 3)] + [dev(y=up(y, d)) for d in (1, 2, 3)]
    for p in partners:
        pl.semaphore_signal(barrier, inc=1, device_id=p, device_id_type=MESH)
    pl.semaphore_wait(barrier, len(partners))

    sems = Sems(send_sem, recv_sem)
    sent = []

    class Copy:
        def __init__(self, tag, landing):
            self.tag, self.landing, self.sems, self.here = tag, landing, sems.take(), False

        def start(self, src, dst, to):
            s, r = self.sems
            cp = pltpu.make_async_remote_copy(src_ref=src, dst_ref=dst, send_sem=s, recv_sem=r,
                                              device_id=to, device_id_type=MESH)
            cp.start()
            sent.append(cp)

        def arrived(self):
            if self.here:
                return
            self.here = True
            s, r = self.sems
            pltpu.make_async_remote_copy(src_ref=self.landing, dst_ref=self.landing, send_sem=s, recv_sem=r,
                                         device_id=dev(), device_id_type=MESH).wait_recv()

    n_local = [0]

    def local(src, dst):
        cp = pltpu.make_async_copy(src, dst, local_sem.at[n_local[0]])
        n_local[0] += 1
        cp.start()
        return cp

    def xa_at(xs, zs):
        return xa.at[pl.ds(pl.multiple_of(xs * (NZ * da) + zs * da, da), da), :]

    def ba_at(ys, core):
        return ba.at[pl.ds(pl.multiple_of(ys * da + core * (da // 2), da // 2), da // 2), :]

    def ba_cols(ys):
        return pl.ds(pl.multiple_of(ys * fa, fa), fa)

    def xg_at(ys, zs):
        return xg.at[ys, pl.ds(pl.multiple_of(zs * dg, 32), dg - flip), :]

    def xv_at(ys, zs):
        return xg.at[ys, pl.ds(pl.multiple_of(zs * dg + (dg - flip), 32), flip), :]

    def bg_at(h, ys, xs):
        return bg.at[ys, pl.ds(pl.multiple_of(NX * at[h] + xs * PARTS[h], 16), PARTS[h]), :]

    def bg_cols(h, ys, xs):
        return basis_g.at[at[h]:at[h] + PARTS[h], pl.ds(pl.multiple_of(ys * fy + xs * fx, 128), fx)]

    def part_rows(h, xs):
        return pl.ds(pl.multiple_of(NX * at[h] + xs * PARTS[h], 16), PARTS[h])

    def rows_of(h):
        return pl.ds(at[h], PARTS[h])

    parts = range(len(PARTS))
    main, rest = grads.at[0:dg - flip, :], grads.at[dg - flip:dg, :]

    def lanes(q):
        return pl.ds(pl.multiple_of(q * quarter, quarter), quarter)

    def sq_block(t, xs, zs, q):
        return sq.at[t, pl.ds(pl.multiple_of((xs * NZ + zs) * da, da), da), lanes(q)]

    def sq_chunk(xs, q, first=0, rows=NZ * da):
        return sq.at[0:SPLIT, pl.ds(pl.multiple_of(xs * (NZ * da) + first, 128), rows), lanes(q)]

    def sq_rest(xs, q):
        return sq.at[SPLIT:NT, pl.ds(pl.multiple_of(xs * (NZ * da), NZ * da), NZ * da), lanes(q)]

    a_z = {d: Copy("a_z", xa_at(x, dn(zl, d))) for d in THREE}
    a_x = {(j, d): Copy("a_x", xa_at(dn(x, d), dn(zl, j))) for j in range(4) for d in SIDES}
    a_f = {j: Copy("a_f", xa_at(up(x, 2), dn(zl, j))) for j in range(4)}
    b_a = {d: Copy("b_a", ba_at(dn(y, d), c)) for d in THREE}
    a_s = {d: Copy("a_s", ba_at(dn(y, d), 1 - c)) for d in THREE}
    p_a = {d: Copy("p_a", ra.at[d - 1]) for d in THREE}
    g_z = {d: Copy("g_z", xg_at(y, dn(zl, d))) for d in THREE}
    g_y = {(j, d): Copy("g_y", xg_at(dn(y, d), dn(zl, j))) for j in range(4) for d in SIDES}
    g_f = {j: Copy("g_f", xg_at(up(y, 2), dn(zl, j))) for j in range(4)}
    v_y = {d: Copy("v_y", xv_at(dn(y, d), zl)) for d in THREE}
    v_z = {(i, d): Copy("v_z", xv_at(dn(y, i), dn(zl, d))) for i in range(4) for d in THREE}
    mine = [up(y, 3 * c), up(y, 1 + c)]
    theirs = [up(y, 3 * (1 - c)), up(y, 2 - c)]
    pieces = [(h, k, d) for h in parts for k in range(2) for d in THREE]
    b_x = {(h, k, d): Copy("b_x", bg_at(h, mine[k], dn(x, d))) for h, k, d in pieces}
    b_s = {(h, k, d): Copy("b_s", bg_at(h, theirs[k], dn(x, d))) for h, k, d in pieces}
    p_g = {(h, d): Copy("p_g", pr.at[d - 1, rows_of(h), :]) for h in parts for d in THREE}
    turns = [(dt, dz) for dt in range(4) for dz in range(4) if dt or dz]
    s_z = {(dt, dz): Copy("s_z", sq_block(dn(tok, dt), x, dn(zl, dz), y)) for dt, dz in turns}
    s_x = {d: Copy("s_x", sq_chunk(dn(x, d), y)) for d in SIDES}
    s_xf = [Copy("s_xf", sq_chunk(up(x, 2), y, 128 * i, 128)) for i in range(2)]
    s_y = {(j, d): Copy("s_y", sq_chunk(dn(x, j), dn(y, d))) for j in range(4) for d in SIDES}
    s_f = {j: Copy("s_f", sq_chunk(dn(x, j), up(y, 2))) for j in range(4)}
    u_y = {d: Copy("u_y", sq_rest(x, dn(y, d))) for d in THREE}
    u_x = {(j, d): Copy("u_x", sq_rest(dn(x, d), dn(y, j))) for j in range(4) for d in SIDES}
    u_f = {j: Copy("u_f", sq_rest(up(x, 2), dn(y, j))) for j in range(4)}

    def sg_at(t, h):
        return sg.at[t, rows_of(h), :]

    t_far = [Copy("t_far", sg_at(far, h)) for h in parts]
    t_sib = [Copy("t_sib", sg_at(sib, h)) for h in parts]
    t_both = [Copy("t_both", sg_at(up(sib, 2), h)) for h in parts]

    def all_of(*groups):
        for group in groups:
            for copy in group.values() if isinstance(group, dict) else group:
                copy.arrived()

    for d in THREE:
        a_z[d].start(acts, xa_at(x, zl), dev(zl=up(zl, d)))
    for d in SIDES:
        a_x[0, d].start(acts, xa_at(x, zl), dev(x=up(x, d)))
    for d in THREE:
        b_a[d].start(basis_a.at[pl.ds(pl.multiple_of(c * (da // 2), da // 2), da // 2), ba_cols(up(y, d))], ba_at(y, c),
                     dev(y=up(y, d)))
    for d in SIDES:
        g_y[0, d].start(main, xg_at(y, zl), dev(y=up(y, d)))
    for d in THREE:
        v_y[d].start(rest, xv_at(y, zl), dev(y=up(y, d)))
    own_a = [local(acts, xa_at(x, zl)), local(basis_a.at[:, ba_cols(y)], ba.at[pl.ds(pl.multiple_of(y * da, da), da), :])]
    own_g = [local(grads, xg.at[y, pl.ds(pl.multiple_of(zl * dg, 32), dg), :])]
    own_g += [local(bg_cols(h, ys, x), bg_at(h, ys, x)) for h in parts for ys in mine + theirs]
    own_s = []

    def ax(j):
        a_z[j].arrived()
        for d in SIDES:
            a_x[j, d].start(xa_at(x, dn(zl, j)), xa_at(x, dn(zl, j)), dev(x=up(x, d)))

    def af(j):
        d = way(j)
        a_x[j, d].arrived()
        a_f[j].start(xa_at(dn(x, d), dn(zl, j)), xa_at(dn(x, d), dn(zl, j)), dev(x=up(x, d)))

    def share_a(d):
        b_a[d].arrived()
        a_s[d].start(ba_at(dn(y, d), c), ba_at(dn(y, d), c), dev(tok=sib))

    def project_a():
        for cp in own_a:
            cp.wait()
        all_of(a_x, a_f, b_a, a_s)
        for ys in range(NY):
            pa[ys] = jnp.dot(ba[...], xa[:, ys * quarter:(ys + 1) * quarter], preferred_element_type=F32)
        for d in THREE:
            p_a[d].start(pa.at[up(y, d)], ra.at[d - 1], dev(y=up(y, d)))

    def square_a():
        all_of(p_a)
        total = pa[y] + ra[0] + ra[1] + ra[2]
        sa[...] = (total * total).astype(BF16)
        for dt, dz in turns:
            t = up(tok, dt)
            s_z[dt, dz].start(sa.at[pl.ds(pl.multiple_of(t * da, da), da), :], sq_block(tok, x, zl, y),
                              dev(tok=t, zl=up(zl, dz)))
        own_s.append(local(sa.at[pl.ds(pl.multiple_of(tok * da, da), da), :], sq_block(tok, x, zl, y)))

    def spread(j):
        for d in SIDES:
            s_y[j, d].start(sq_chunk(dn(x, j), y), sq_chunk(dn(x, j), y), dev(y=up(y, d)))

    def spread_rest(j):
        for d in SIDES:
            u_x[j, d].start(sq_rest(x, dn(y, j)), sq_rest(x, dn(y, j)), dev(x=up(x, d)))

    def sx():
        own_s[0].wait()
        all_of(s_z)
        for d in SIDES:
            s_x[d].start(sq_chunk(x, y), sq_chunk(x, y), dev(x=up(x, d)))
        spread(0)
        for d in THREE:
            u_y[d].start(sq_rest(x, y), sq_rest(x, y), dev(y=up(y, d)))
        spread_rest(0)

    def sxf(i):
        d = SIDES[i]
        s_x[d].arrived()
        part = sq_chunk(dn(x, d), y, 128 * i, 128)
        s_xf[i].start(part, part, dev(x=up(x, d)))

    def ss(j):
        all_of(s_xf if j == 2 else [s_x[j]])
        spread(j)

    def sf(j):
        d = way(j)
        s_y[j, d].arrived()
        s_f[j].start(sq_chunk(dn(x, j), dn(y, d)), sq_chunk(dn(x, j), dn(y, d)), dev(y=up(y, d)))

    def us(j):
        u_y[j].arrived()
        spread_rest(j)

    def uf(j):
        d = way(j)
        u_x[j, d].arrived()
        u_f[j].start(sq_rest(dn(x, d), dn(y, j)), sq_rest(dn(x, d), dn(y, j)), dev(x=up(x, d)))

    def gz(d):
        g_z[d].start(main, xg_at(y, zl), dev(zl=up(zl, d)))

    def gs(j):
        g_z[j].arrived()
        for d in SIDES:
            g_y[j, d].start(xg_at(y, dn(zl, j)), xg_at(y, dn(zl, j)), dev(y=up(y, d)))

    def gf(j):
        d = way(j)
        g_y[j, d].arrived()
        g_f[j].start(xg_at(dn(y, d), dn(zl, j)), xg_at(dn(y, d), dn(zl, j)), dev(y=up(y, d)))

    def vz(i):
        if i:
            v_y[i].arrived()
        for d in THREE:
            v_z[i, d].start(xv_at(dn(y, i), zl) if i else rest, xv_at(dn(y, i), zl), dev(zl=up(zl, d)))

    def bx(h, k, d):
        b_x[h, k, d].start(bg_cols(h, mine[k], up(x, d)), bg_at(h, mine[k], x), dev(x=up(x, d)))

    def bs(h, k, d):
        b_x[h, k, d].arrived()
        b_s[h, k, d].start(bg_at(h, mine[k], dn(x, d)), bg_at(h, mine[k], dn(x, d)), dev(tok=sib))

    def cg(h, i):
        while own_g:
            own_g.pop().wait()
        for d in THREE:
            all_of([b_x[h, i // 2, d], b_s[h, i // 2, d]])
        ring = (0, 1, 3, 2)[i]
        if i == 0:
            all_of(g_z)
        elif i == 3:
            all_of(g_f)
        else:
            all_of([g_y[j, ring] for j in range(4)])
        all_of([v_z[ring, d] for d in THREE], [v_y[ring]] if ring else [])
        ys = dn(y, ring)
        rows = slice(NX * at[h], NX * (at[h] + PARTS[h]))
        part = jnp.dot(bg[ys, rows, :], xg[ys], preferred_element_type=F32)
        acc[rows, :] = part if i == 0 else acc[rows, :] + part
        if i == 3:
            ps[rows, :] = acc[rows, :].astype(BF16)
            for d in (2, 1, 3):
                xs = up(x, d)
                p_g[h, d].start(ps.at[part_rows(h, xs), :], pr.at[d - 1, rows_of(h), :], dev(x=xs))

    def square_g(h):
        all_of([p_g[h, d] for d in THREE])
        total = acc[part_rows(h, x), :]
        for d in range(NX - 1):
            total = total + pr[d, rows_of(h), :].astype(F32)
        sg[tok, rows_of(h), :] = (total * total).astype(BF16)
        t_far[h].start(sg_at(tok, h), sg_at(tok, h), dev(tok=far))
        t_sib[h].start(sg_at(tok, h), sg_at(tok, h), dev(tok=sib))

    def tb(h):
        t_far[h].arrived()
        t_both[h].start(sg_at(far, h), sg_at(far, h), dev(tok=sib))

    tile = 256
    scale = 1.0 / (cols * NT)

    def fin(i):
        all_of(*((s_x, s_xf, s_y, s_f, u_y, u_x, u_f), (t_sib,), (t_far,), (t_both,))[i])
        t = (tok, sib, far, up(sib, 2))[i]
        for n in range(0, out.shape[1], tile):
            part = lax.dot_general(sg[t], sq[t, n:n + tile, :], (((1,), (1,)), ((), ())), preferred_element_type=F32)
            value = part if i == 0 else out[:, n:n + tile] + part
            out[:, n:n + tile] = value * scale if i == 3 else value

    steps = {"ax": ax, "af": af, "as": share_a, "pa": project_a, "sa": square_a, "sx": sx, "sxf": sxf, "ss": ss, "sf": sf,
             "us": us, "uf": uf, "gz": gz, "gs": gs, "gf": gf, "vz": vz, "bx": bx, "bs": bs, "cg": cg, "sq": square_g, "tb": tb,
             "fin": fin}
    for name, *where in SCHEDULE:
        steps[name](*where)

    for cp in sent:
        cp.wait_send()


def body(acts_t, grads_t, basis_a, basis_g):
    da, cols = acts_t.shape
    dg = grads_t.shape[0]
    fa = basis_a.shape[1] // NY
    rows_a, quarter = NY * da, cols // NY
    fx = NZ * dg
    anywhere = pl.BlockSpec(memory_space=pl.ANY)
    n_out = basis_a.shape[1] // NT
    return pl.pallas_call(
        kernel,
        out_shape=jax.ShapeDtypeStruct((dg, n_out), F32),
        in_specs=[anywhere] * 4,
        out_specs=pl.BlockSpec(memory_space=pltpu.VMEM),
        scratch_shapes=[
            pltpu.VMEM((fa, cols), BF16),
            pltpu.VMEM((rows_a, fa), BF16),
            pltpu.VMEM((NY, rows_a, quarter), F32),
            pltpu.VMEM((NY - 1, rows_a, quarter), F32),
            pltpu.VMEM((rows_a, quarter), BF16),
            pltpu.VMEM((NT, n_out, cols), BF16),
            pltpu.VMEM((NY, fx, cols), BF16),
            pltpu.VMEM((NY, NX * dg, fx), BF16),
            pltpu.VMEM((NX * dg, cols), F32),
            pltpu.VMEM((NX * dg, cols), BF16),
            pltpu.VMEM((NX - 1, dg, cols), BF16),
            pltpu.VMEM((NT, dg, cols), BF16),
            pltpu.SemaphoreType.DMA((N_COPIES,)),
            pltpu.SemaphoreType.DMA((N_COPIES,)),
            pltpu.SemaphoreType.DMA((N_LOCAL,)),
        ],
        compiler_params=pltpu.CompilerParams(
            collective_id=0, has_side_effects=True, vmem_limit_bytes=60 * 2**20
        ),
    )(acts_t, grads_t, basis_a, basis_g)


def solution(mesh):
    return jax.shard_map(
        body,
        mesh=mesh,
        in_specs=(P("col", "tok"), P("col", "tok"), P("col", None), P("col", None)),
        out_specs=P("col", "tok"),
        check_vma=False,
    )
```

```python
import jax
import jax.numpy as jnp
from jax import lax
from jax.experimental import pallas as pl
from jax.experimental.pallas import tpu as pltpu
from jax.sharding import PartitionSpec as P

MESH = pl.DeviceIdType.MESH
BF16 = jnp.bfloat16
F32 = jnp.float32
NX, NY, NZ, NT = 4, 4, 4, 4


class Sems:
    def __init__(self, send, recv):
        self.send, self.recv, self.used = send, recv, 0

    def take(self):
        i = self.used
        self.used += 1
        return self.send.at[i], self.recv.at[i]


N_COPIES = 160
N_LOCAL = 24

THREE = (1, 3, 2)
SIDES = (1, 3)


def way(j):
    return 1 if j < 2 else 3


SCHEDULE = (
    ("gz", 3), ("bx", 2, 0, 2), ("bx", 2, 0, 3), ("bx", 1, 1, 1), ("bx", 0, 0, 1), ("bx", 0, 0, 3), ("ax", 2),
    ("as", 1), ("as", 2), ("bs", 2, 0, 3), ("gz", 2), ("ax", 3), ("gf", 0), ("ax", 1), ("af", 2), ("af", 3),
    ("af", 0), ("vz", 0), ("bs", 2, 0, 2), ("bx", 0, 1, 2), ("af", 1), ("as", 3), ("gs", 3), ("gz", 1),
    ("bs", 0, 0, 1), ("bx", 1, 1, 3), ("gs", 2), ("bx", 1, 0, 3), ("bx", 0, 1, 1), ("bx", 2, 0, 1), ("pa",),
    ("bx", 2, 1, 1), ("bx", 2, 1, 3), ("bs", 0, 1, 2), ("vz", 1), ("bs", 2, 0, 1), ("bx", 0, 1, 3), ("bx", 1, 0, 1),
    ("bs", 1, 1, 3), ("cg", 2, 0), ("gs", 1), ("bx", 1, 1, 2), ("gf", 2), ("bx", 2, 1, 2), ("bs", 2, 1, 3),
    ("bx", 1, 0, 2), ("bs", 0, 0, 3), ("sa",), ("gf", 3), ("gf", 1), ("bs", 0, 1, 3), ("vz", 3), ("sx",),
    ("bs", 1, 1, 1), ("vz", 2), ("cg", 2, 1), ("bs", 1, 0, 3), ("bs", 1, 0, 2), ("bs", 1, 0, 1), ("cg", 1, 0),
    ("bs", 2, 1, 1), ("bx", 0, 0, 2), ("bs", 1, 1, 2), ("bs", 2, 1, 2), ("ss", 3), ("cg", 1, 1), ("bs", 0, 1, 1),
    ("ss", 1), ("us", 1), ("cg", 1, 2), ("sxf", 1), ("sf", 0), ("sxf", 0), ("cg", 2, 2), ("bs", 0, 0, 2),
    ("cg", 2, 3), ("cg", 1, 3), ("cg", 0, 0), ("cg", 0, 1), ("ss", 2), ("cg", 0, 2), ("cg", 0, 3), ("sq", 2),
    ("sf", 3), ("sq", 1), ("sf", 1), ("us", 3), ("sf", 2), ("tb", 2), ("uf", 1), ("us", 2), ("sq", 0), ("uf", 3),
    ("tb", 1), ("uf", 0), ("uf", 2), ("tb", 0), ("fin", 0), ("fin", 1), ("fin", 2), ("fin", 3),
)


SPLIT = 3
PARTS = (96, 80, 48)
FLIP = 64


def kernel(acts, grads, basis_a, basis_g, out, xa, ba, pa, ra, sa, sq, xg, bg, acc, ps, pr, sg,
           send_sem, recv_sem, local_sem):
    tok = lax.axis_index("tok")
    col = lax.axis_index("col")
    zl = lax.rem(col, 4)
    x = lax.rem(lax.div(col, 4), 4)
    y = lax.div(col, 16)
    c = lax.rem(tok, 2)
    da, fa = acts.shape[0], basis_a.shape[1] // NY
    dg = grads.shape[0]
    at = [sum(PARTS[:h]) for h in range(len(PARTS))]
    flip = FLIP
    fx = NZ * dg
    fy = NX * fx
    cols = acts.shape[1]
    quarter = cols // NY

    def up(v, d):
        return lax.rem(v + d, 4)

    def dn(v, d):
        return lax.rem(v + 4 - d, 4)

    def dev(tok=tok, y=y, x=x, zl=zl):
        return (tok, (y * 4 + x) * 4 + zl)

    sib = tok + 1 - 2 * c
    far = up(tok, 2)

    barrier = pltpu.get_barrier_semaphore()
    partners = [dev(tok=up(tok, dt), zl=up(zl, dz)) for dt in range(4) for dz in range(4) if dt or dz]
    partners += [dev(x=up(x, d)) for d in (1, 2, 3)] + [dev(y=up(y, d)) for d in (1, 2, 3)]
    for p in partners:
        pl.semaphore_signal(barrier, inc=1, device_id=p, device_id_type=MESH)
    pl.semaphore_wait(barrier, len(partners))

    sems = Sems(send_sem, recv_sem)
    sent = []

    class Copy:
        def __init__(self, tag, landing):
            self.tag, self.landing, self.sems, self.here = tag, landing, sems.take(), False

        def start(self, src, dst, to):
            s, r = self.sems
            cp = pltpu.make_async_remote_copy(src_ref=src, dst_ref=dst, send_sem=s, recv_sem=r,
                                              device_id=to, device_id_type=MESH)
            cp.start()
            sent.append(cp)

        def arrived(self):
            if self.here:
                return
            self.here = True
            s, r = self.sems
            pltpu.make_async_remote_copy(src_ref=self.landing, dst_ref=self.landing, send_sem=s, recv_sem=r,
                                         device_id=dev(), device_id_type=MESH).wait_recv()

    n_local = [0]

    def local(src, dst):
        cp = pltpu.make_async_copy(src, dst, local_sem.at[n_local[0]])
        n_local[0] += 1
        cp.start()
        return cp

    def xa_at(xs, zs):
        return xa.at[pl.ds(pl.multiple_of(xs * (NZ * da) + zs * da, da), da), :]

    def ba_at(ys, core):
        return ba.at[pl.ds(pl.multiple_of(ys * da + core * (da // 2), da // 2), da // 2), :]

    def ba_cols(ys):
        return pl.ds(pl.multiple_of(ys * fa, fa), fa)

    def xg_at(ys, zs):
        return xg.at[ys, pl.ds(pl.multiple_of(zs * dg, 32), dg - flip), :]

    def xv_at(ys, zs):
        return xg.at[ys, pl.ds(pl.multiple_of(zs * dg + (dg - flip), 32), flip), :]

    def bg_at(h, ys, xs):
        return bg.at[ys, pl.ds(pl.multiple_of(NX * at[h] + xs * PARTS[h], 16), PARTS[h]), :]

    def bg_cols(h, ys, xs):
        return basis_g.at[at[h]:at[h] + PARTS[h], pl.ds(pl.multiple_of(ys * fy + xs * fx, 128), fx)]

    def part_rows(h, xs):
        return pl.ds(pl.multiple_of(NX * at[h] + xs * PARTS[h], 16), PARTS[h])

    def rows_of(h):
        return pl.ds(at[h], PARTS[h])

    parts = range(len(PARTS))
    main, rest = grads.at[0:dg - flip, :], grads.at[dg - flip:dg, :]

    def lanes(q):
        return pl.ds(pl.multiple_of(q * quarter, quarter), quarter)

    def sq_block(t, xs, zs, q):
        return sq.at[t, pl.ds(pl.multiple_of((xs * NZ + zs) * da, da), da), lanes(q)]

    def sq_chunk(xs, q, first=0, rows=NZ * da):
        return sq.at[0:SPLIT, pl.ds(pl.multiple_of(xs * (NZ * da) + first, 128), rows), lanes(q)]

    def sq_rest(xs, q):
        return sq.at[SPLIT:NT, pl.ds(pl.multiple_of(xs * (NZ * da), NZ * da), NZ * da), lanes(q)]

    a_z = {d: Copy("a_z", xa_at(x, dn(zl, d))) for d in THREE}
    a_x = {(j, d): Copy("a_x", xa_at(dn(x, d), dn(zl, j))) for j in range(4) for d in SIDES}
    a_f = {j: Copy("a_f", xa_at(up(x, 2), dn(zl, j))) for j in range(4)}
    b_a = {d: Copy("b_a", ba_at(dn(y, d), c)) for d in THREE}
    a_s = {d: Copy("a_s", ba_at(dn(y, d), 1 - c)) for d in THREE}
    p_a = {d: Copy("p_a", ra.at[d - 1]) for d in THREE}
    g_z = {d: Copy("g_z", xg_at(y, dn(zl, d))) for d in THREE}
    g_y = {(j, d): Copy("g_y", xg_at(dn(y, d), dn(zl, j))) for j in range(4) for d in SIDES}
    g_f = {j: Copy("g_f", xg_at(up(y, 2), dn(zl, j))) for j in range(4)}
    v_y = {d: Copy("v_y", xv_at(dn(y, d), zl)) for d in THREE}
    v_z = {(i, d): Copy("v_z", xv_at(dn(y, i), dn(zl, d))) for i in range(4) for d in THREE}
    mine = [up(y, 3 * c), up(y, 1 + c)]
    theirs = [up(y, 3 * (1 - c)), up(y, 2 - c)]
    pieces = [(h, k, d) for h in parts for k in range(2) for d in THREE]
    b_x = {(h, k, d): Copy("b_x", bg_at(h, mine[k], dn(x, d))) for h, k, d in pieces}
    b_s = {(h, k, d): Copy("b_s", bg_at(h, theirs[k], dn(x, d))) for h, k, d in pieces}
    p_g = {(h, d): Copy("p_g", pr.at[d - 1, rows_of(h), :]) for h in parts for d in THREE}
    turns = [(dt, dz) for dt in range(4) for dz in range(4) if dt or dz]
    s_z = {(dt, dz): Copy("s_z", sq_block(dn(tok, dt), x, dn(zl, dz), y)) for dt, dz in turns}
    s_x = {d: Copy("s_x", sq_chunk(dn(x, d), y)) for d in SIDES}
    s_xf = [Copy("s_xf", sq_chunk(up(x, 2), y, 128 * i, 128)) for i in range(2)]
    s_y = {(j, d): Copy("s_y", sq_chunk(dn(x, j), dn(y, d))) for j in range(4) for d in SIDES}
    s_f = {j: Copy("s_f", sq_chunk(dn(x, j), up(y, 2))) for j in range(4)}
    u_y = {d: Copy("u_y", sq_rest(x, dn(y, d))) for d in THREE}
    u_x = {(j, d): Copy("u_x", sq_rest(dn(x, d), dn(y, j))) for j in range(4) for d in SIDES}
    u_f = {j: Copy("u_f", sq_rest(up(x, 2), dn(y, j))) for j in range(4)}

    def sg_at(t, h):
        return sg.at[t, rows_of(h), :]

    t_far = [Copy("t_far", sg_at(far, h)) for h in parts]
    t_sib = [Copy("t_sib", sg_at(sib, h)) for h in parts]
    t_both = [Copy("t_both", sg_at(up(sib, 2), h)) for h in parts]

    def all_of(*groups):
        for group in groups:
            for copy in group.values() if isinstance(group, dict) else group:
                copy.arrived()

    for d in THREE:
        a_z[d].start(acts, xa_at(x, zl), dev(zl=up(zl, d)))
    for d in SIDES:
        a_x[0, d].start(acts, xa_at(x, zl), dev(x=up(x, d)))
    for d in THREE:
        b_a[d].start(basis_a.at[pl.ds(pl.multiple_of(c * (da // 2), da // 2), da // 2), ba_cols(up(y, d))], ba_at(y, c),
                     dev(y=up(y, d)))
    for d in SIDES:
        g_y[0, d].start(main, xg_at(y, zl), dev(y=up(y, d)))
    for d in THREE:
        v_y[d].start(rest, xv_at(y, zl), dev(y=up(y, d)))
    own_a = [local(acts, xa_at(x, zl)), local(basis_a.at[:, ba_cols(y)], ba.at[pl.ds(pl.multiple_of(y * da, da), da), :])]
    own_g = [local(grads, xg.at[y, pl.ds(pl.multiple_of(zl * dg, 32), dg), :])]
    own_g += [local(bg_cols(h, ys, x), bg_at(h, ys, x)) for h in parts for ys in mine + theirs]
    own_s = []

    def ax(j):
        a_z[j].arrived()
        for d in SIDES:
            a_x[j, d].start(xa_at(x, dn(zl, j)), xa_at(x, dn(zl, j)), dev(x=up(x, d)))

    def af(j):
        d = way(j)
        a_x[j, d].arrived()
        a_f[j].start(xa_at(dn(x, d), dn(zl, j)), xa_at(dn(x, d), dn(zl, j)), dev(x=up(x, d)))

    def share_a(d):
        b_a[d].arrived()
        a_s[d].start(ba_at(dn(y, d), c), ba_at(dn(y, d), c), dev(tok=sib))

    def project_a():
        for cp in own_a:
            cp.wait()
        all_of(a_x, a_f, b_a, a_s)
        for ys in range(NY):
            pa[ys] = jnp.dot(ba[...], xa[:, ys * quarter:(ys + 1) * quarter], preferred_element_type=F32)
        for d in THREE:
            p_a[d].start(pa.at[up(y, d)], ra.at[d - 1], dev(y=up(y, d)))

    def square_a():
        all_of(p_a)
        total = pa[y] + ra[0] + ra[1] + ra[2]
        sa[...] = (total * total).astype(BF16)
        for dt, dz in turns:
            t = up(tok, dt)
            s_z[dt, dz].start(sa.at[pl.ds(pl.multiple_of(t * da, da), da), :], sq_block(tok, x, zl, y),
                              dev(tok=t, zl=up(zl, dz)))
        own_s.append(local(sa.at[pl.ds(pl.multiple_of(tok * da, da), da), :], sq_block(tok, x, zl, y)))

    def spread(j):
        for d in SIDES:
            s_y[j, d].start(sq_chunk(dn(x, j), y), sq_chunk(dn(x, j), y), dev(y=up(y, d)))

    def spread_rest(j):
        for d in SIDES:
            u_x[j, d].start(sq_rest(x, dn(y, j)), sq_rest(x, dn(y, j)), dev(x=up(x, d)))

    def sx():
        own_s[0].wait()
        all_of(s_z)
        for d in SIDES:
            s_x[d].start(sq_chunk(x, y), sq_chunk(x, y), dev(x=up(x, d)))
        spread(0)
        for d in THREE:
            u_y[d].start(sq_rest(x, y), sq_rest(x, y), dev(y=up(y, d)))
        spread_rest(0)

    def sxf(i):
        d = SIDES[i]
        s_x[d].arrived()
        part = sq_chunk(dn(x, d), y, 128 * i, 128)
        s_xf[i].start(part, part, dev(x=up(x, d)))

    def ss(j):
        all_of(s_xf if j == 2 else [s_x[j]])
        spread(j)

    def sf(j):
        d = way(j)
        s_y[j, d].arrived()
        s_f[j].start(sq_chunk(dn(x, j), dn(y, d)), sq_chunk(dn(x, j), dn(y, d)), dev(y=up(y, d)))

    def us(j):
        u_y[j].arrived()
        spread_rest(j)

    def uf(j):
        d = way(j)
        u_x[j, d].arrived()
        u_f[j].start(sq_rest(dn(x, d), dn(y, j)), sq_rest(dn(x, d), dn(y, j)), dev(x=up(x, d)))

    def gz(d):
        g_z[d].start(main, xg_at(y, zl), dev(zl=up(zl, d)))

    def gs(j):
        g_z[j].arrived()
        for d in SIDES:
            g_y[j, d].start(xg_at(y, dn(zl, j)), xg_at(y, dn(zl, j)), dev(y=up(y, d)))

    def gf(j):
        d = way(j)
        g_y[j, d].arrived()
        g_f[j].start(xg_at(dn(y, d), dn(zl, j)), xg_at(dn(y, d), dn(zl, j)), dev(y=up(y, d)))

    def vz(i):
        if i:
            v_y[i].arrived()
        for d in THREE:
            v_z[i, d].start(xv_at(dn(y, i), zl) if i else rest, xv_at(dn(y, i), zl), dev(zl=up(zl, d)))

    def bx(h, k, d):
        b_x[h, k, d].start(bg_cols(h, mine[k], up(x, d)), bg_at(h, mine[k], x), dev(x=up(x, d)))

    def bs(h, k, d):
        b_x[h, k, d].arrived()
        b_s[h, k, d].start(bg_at(h, mine[k], dn(x, d)), bg_at(h, mine[k], dn(x, d)), dev(tok=sib))

    def cg(h, i):
        while own_g:
            own_g.pop().wait()
        for d in THREE:
            all_of([b_x[h, i // 2, d], b_s[h, i // 2, d]])
        ring = (0, 1, 3, 2)[i]
        if i == 0:
            all_of(g_z)
        elif i == 3:
            all_of(g_f)
        else:
            all_of([g_y[j, ring] for j in range(4)])
        all_of([v_z[ring, d] for d in THREE], [v_y[ring]] if ring else [])
        ys = dn(y, ring)
        rows = slice(NX * at[h], NX * (at[h] + PARTS[h]))
        part = jnp.dot(bg[ys, rows, :], xg[ys], preferred_element_type=F32)
        acc[rows, :] = part if i == 0 else acc[rows, :] + part
        if i == 3:
            ps[rows, :] = acc[rows, :].astype(BF16)
            for d in (2, 1, 3):
                xs = up(x, d)
                p_g[h, d].start(ps.at[part_rows(h, xs), :], pr.at[d - 1, rows_of(h), :], dev(x=xs))

    def square_g(h):
        all_of([p_g[h, d] for d in THREE])
        total = acc[part_rows(h, x), :]
        for d in range(NX - 1):
            total = total + pr[d, rows_of(h), :].astype(F32)
        sg[tok, rows_of(h), :] = (total * total).astype(BF16)
        t_far[h].start(sg_at(tok, h), sg_at(tok, h), dev(tok=far))
        t_sib[h].start(sg_at(tok, h), sg_at(tok, h), dev(tok=sib))

    def tb(h):
        t_far[h].arrived()
        t_both[h].start(sg_at(far, h), sg_at(far, h), dev(tok=sib))

    tile = 256
    scale = 1.0 / (cols * NT)

    def fin(i):
        all_of(*((s_x, s_xf, s_y, s_f, u_y, u_x, u_f), (t_sib,), (t_far,), (t_both,))[i])
        t = (tok, sib, far, up(sib, 2))[i]
        for n in range(0, out.shape[1], tile):
            part = lax.dot_general(sg[t], sq[t, n:n + tile, :], (((1,), (1,)), ((), ())), preferred_element_type=F32)
            value = part if i == 0 else out[:, n:n + tile] + part
            out[:, n:n + tile] = value * scale if i == 3 else value

    steps = {"ax": ax, "af": af, "as": share_a, "pa": project_a, "sa": square_a, "sx": sx, "sxf": sxf, "ss": ss, "sf": sf,
             "us": us, "uf": uf, "gz": gz, "gs": gs, "gf": gf, "vz": vz, "bx": bx, "bs": bs, "cg": cg, "sq": square_g, "tb": tb,
             "fin": fin}
    for name, *where in SCHEDULE:
        steps[name](*where)

    for cp in sent:
        cp.wait_send()


def body(acts_t, grads_t, basis_a, basis_g):
    da, cols = acts_t.shape
    dg = grads_t.shape[0]
    fa = basis_a.shape[1] // NY
    rows_a, quarter = NY * da, cols // NY
    fx = NZ * dg
    anywhere = pl.BlockSpec(memory_space=pl.ANY)
    n_out = basis_a.shape[1] // NT
    return pl.pallas_call(
        kernel,
        out_shape=jax.ShapeDtypeStruct((dg, n_out), F32),
        in_specs=[anywhere] * 4,
        out_specs=pl.BlockSpec(memory_space=pltpu.VMEM),
        scratch_shapes=[
            pltpu.VMEM((fa, cols), BF16),
            pltpu.VMEM((rows_a, fa), BF16),
            pltpu.VMEM((NY, rows_a, quarter), F32),
            pltpu.VMEM((NY - 1, rows_a, quarter), F32),
            pltpu.VMEM((rows_a, quarter), BF16),
            pltpu.VMEM((NT, n_out, cols), BF16),
            pltpu.VMEM((NY, fx, cols), BF16),
            pltpu.VMEM((NY, NX * dg, fx), BF16),
            pltpu.VMEM((NX * dg, cols), F32),
            pltpu.VMEM((NX * dg, cols), BF16),
            pltpu.VMEM((NX - 1, dg, cols), BF16),
            pltpu.VMEM((NT, dg, cols), BF16),
            pltpu.SemaphoreType.DMA((N_COPIES,)),
            pltpu.SemaphoreType.DMA((N_COPIES,)),
            pltpu.SemaphoreType.DMA((N_LOCAL,)),
        ],
        compiler_params=pltpu.CompilerParams(
            collective_id=0, has_side_effects=True, vmem_limit_bytes=60 * 2**20
        ),
    )(acts_t, grads_t, basis_a, basis_g)


def solution(mesh):
    return jax.shard_map(
        body,
        mesh=mesh,
        in_specs=(P("col", "tok"), P("col", "tok"), P("col", None), P("col", None)),
        out_specs=P("col", "tok"),
        check_vma=False,
    )
```

```python
import jax
import jax.numpy as jnp
from jax import lax
from jax.experimental import pallas as pl
from jax.experimental.pallas import tpu as pltpu
from jax.sharding import PartitionSpec as P

MESH = pl.DeviceIdType.MESH
BF16 = jnp.bfloat16
F32 = jnp.float32
NX, NY, NZ, NT = 4, 4, 4, 4


class Sems:
    def __init__(self, send, recv):
        self.send, self.recv, self.used = send, recv, 0

    def take(self):
        i = self.used
        self.used += 1
        return self.send.at[i], self.recv.at[i]


N_COPIES = 160
N_LOCAL = 24

THREE = (1, 3, 2)
SIDES = (1, 3)


def way(j):
    return 1 if j < 2 else 3


SCHEDULE = (
    ("bx", 0, 0, 2), ("ax", 1), ("gz", 2), ("ax", 3), ("gf", 0), ("ax", 2), ("af", 0), ("af", 3), ("af", 1),
    ("as", 3), ("af", 2), ("vz", 0), ("gs", 2), ("as", 2), ("bx", 0, 0, 1), ("gz", 1), ("bx", 0, 0, 3),
    ("bx", 1, 0, 1), ("bs", 0, 0, 2), ("as", 1), ("pa",), ("bx", 1, 0, 3), ("gf", 2), ("gz", 3), ("bx", 0, 1, 1),
    ("bx", 0, 1, 3), ("gs", 1), ("bs", 0, 0, 1), ("bx", 1, 1, 2), ("sa",), ("gs", 3), ("bx", 0, 1, 2),
    ("bs", 0, 0, 3), ("bs", 0, 1, 3), ("sx",), ("bs", 0, 1, 1), ("vz", 3), ("vz", 1), ("bs", 0, 1, 2), ("gf", 3),
    ("gf", 1), ("bx", 1, 0, 2), ("cg", 0, 0), ("vz", 2), ("sxf", 1), ("sxf", 0), ("bs", 1, 1, 2), ("bx", 1, 1, 3),
    ("bs", 1, 0, 3), ("bs", 1, 0, 1), ("cg", 0, 1), ("ss", 3), ("bx", 1, 1, 1), ("cg", 0, 2), ("cg", 0, 3),
    ("bs", 1, 0, 2), ("ss", 2), ("bs", 1, 1, 1), ("ss", 1), ("cg", 1, 0), ("sf", 3), ("cg", 1, 1), ("bs", 1, 1, 3),
    ("cg", 1, 2), ("us", 2), ("sf", 0), ("us", 1), ("cg", 1, 3), ("us", 3), ("sq", 0), ("sf", 2), ("sf", 1),
    ("uf", 1), ("uf", 2), ("sq", 1), ("uf", 3), ("uf", 0), ("tb", 0), ("fin", 0), ("tb", 1), ("fin", 1), ("fin", 2),
    ("fin", 3),
)


SPLIT = 3
PARTS = (160, 64)
FLIP = 32


def kernel(acts, grads, basis_a, basis_g, out, xa, ba, pa, ra, sa, sq, xg, bg, acc, ps, pr, sg,
           send_sem, recv_sem, local_sem):
    tok = lax.axis_index("tok")
    col = lax.axis_index("col")
    zl = lax.rem(col, 4)
    x = lax.rem(lax.div(col, 4), 4)
    y = lax.div(col, 16)
    c = lax.rem(tok, 2)
    da, fa = acts.shape[0], basis_a.shape[1] // NY
    dg = grads.shape[0]
    at = [sum(PARTS[:h]) for h in range(len(PARTS))]
    flip = FLIP
    fx = NZ * dg
    fy = NX * fx
    cols = acts.shape[1]
    quarter = cols // NY

    def up(v, d):
        return lax.rem(v + d, 4)

    def dn(v, d):
        return lax.rem(v + 4 - d, 4)

    def dev(tok=tok, y=y, x=x, zl=zl):
        return (tok, (y * 4 + x) * 4 + zl)

    sib = tok + 1 - 2 * c
    far = up(tok, 2)

    barrier = pltpu.get_barrier_semaphore()
    partners = [dev(tok=up(tok, dt), zl=up(zl, dz)) for dt in range(4) for dz in range(4) if dt or dz]
    partners += [dev(x=up(x, d)) for d in (1, 2, 3)] + [dev(y=up(y, d)) for d in (1, 2, 3)]
    for p in partners:
        pl.semaphore_signal(barrier, inc=1, device_id=p, device_id_type=MESH)
    pl.semaphore_wait(barrier, len(partners))

    sems = Sems(send_sem, recv_sem)
    sent = []

    class Copy:
        def __init__(self, tag, landing):
            self.tag, self.landing, self.sems, self.here = tag, landing, sems.take(), False

        def start(self, src, dst, to):
            s, r = self.sems
            cp = pltpu.make_async_remote_copy(src_ref=src, dst_ref=dst, send_sem=s, recv_sem=r,
                                              device_id=to, device_id_type=MESH)
            cp.start()
            sent.append(cp)

        def arrived(self):
            if self.here:
                return
            self.here = True
            s, r = self.sems
            pltpu.make_async_remote_copy(src_ref=self.landing, dst_ref=self.landing, send_sem=s, recv_sem=r,
                                         device_id=dev(), device_id_type=MESH).wait_recv()

    n_local = [0]

    def local(src, dst):
        cp = pltpu.make_async_copy(src, dst, local_sem.at[n_local[0]])
        n_local[0] += 1
        cp.start()
        return cp

    def xa_at(xs, zs):
        return xa.at[pl.ds(pl.multiple_of(xs * (NZ * da) + zs * da, da), da), :]

    def ba_at(ys, core):
        return ba.at[pl.ds(pl.multiple_of(ys * da + core * (da // 2), da // 2), da // 2), :]

    def ba_cols(ys):
        return pl.ds(pl.multiple_of(ys * fa, fa), fa)

    def xg_at(ys, zs):
        return xg.at[ys, pl.ds(pl.multiple_of(zs * dg, 32), dg - flip), :]

    def xv_at(ys, zs):
        return xg.at[ys, pl.ds(pl.multiple_of(zs * dg + (dg - flip), 32), flip), :]

    def bg_at(h, ys, xs):
        return bg.at[ys, pl.ds(pl.multiple_of(NX * at[h] + xs * PARTS[h], 16), PARTS[h]), :]

    def bg_cols(h, ys, xs):
        return basis_g.at[at[h]:at[h] + PARTS[h], pl.ds(pl.multiple_of(ys * fy + xs * fx, 128), fx)]

    def part_rows(h, xs):
        return pl.ds(pl.multiple_of(NX * at[h] + xs * PARTS[h], 16), PARTS[h])

    def rows_of(h):
        return pl.ds(at[h], PARTS[h])

    parts = range(len(PARTS))
    main, rest = grads.at[0:dg - flip, :], grads.at[dg - flip:dg, :]

    def lanes(t):
        return pl.ds(pl.multiple_of(t * quarter, quarter), quarter)

    def sq_block(t, xs, zs, q):
        return sq.at[q, pl.ds(pl.multiple_of((xs * NZ + zs) * da, da), da), lanes(t)]

    def sq_chunk(xs, q, first=0, rows=NZ * da):
        return sq.at[q, pl.ds(pl.multiple_of(xs * (NZ * da) + first, 128), rows), 0:SPLIT * quarter]

    def sq_rest(xs, q):
        return sq.at[q, pl.ds(pl.multiple_of(xs * (NZ * da), NZ * da), NZ * da), SPLIT * quarter:NT * quarter]

    a_z = {d: Copy("a_z", xa_at(x, dn(zl, d))) for d in THREE}
    a_x = {(j, d): Copy("a_x", xa_at(dn(x, d), dn(zl, j))) for j in range(4) for d in SIDES}
    a_f = {j: Copy("a_f", xa_at(up(x, 2), dn(zl, j))) for j in range(4)}
    b_a = {d: Copy("b_a", ba_at(dn(y, d), c)) for d in THREE}
    a_s = {d: Copy("a_s", ba_at(dn(y, d), 1 - c)) for d in THREE}
    p_a = {d: Copy("p_a", ra.at[d - 1]) for d in THREE}
    g_z = {d: Copy("g_z", xg_at(y, dn(zl, d))) for d in THREE}
    g_y = {(j, d): Copy("g_y", xg_at(dn(y, d), dn(zl, j))) for j in range(4) for d in SIDES}
    g_f = {j: Copy("g_f", xg_at(up(y, 2), dn(zl, j))) for j in range(4)}
    v_y = {d: Copy("v_y", xv_at(dn(y, d), zl)) for d in THREE}
    v_z = {(i, d): Copy("v_z", xv_at(dn(y, i), dn(zl, d))) for i in range(4) for d in THREE}
    mine = [up(y, 3 * c), up(y, 1 + c)]
    theirs = [up(y, 3 * (1 - c)), up(y, 2 - c)]
    pieces = [(h, k, d) for h in parts for k in range(2) for d in THREE]
    b_x = {(h, k, d): Copy("b_x", bg_at(h, mine[k], dn(x, d))) for h, k, d in pieces}
    b_s = {(h, k, d): Copy("b_s", bg_at(h, theirs[k], dn(x, d))) for h, k, d in pieces}
    p_g = {(h, d): Copy("p_g", pr.at[d - 1, rows_of(h), :]) for h in parts for d in THREE}
    turns = [(dt, dz) for dt in range(4) for dz in range(4) if dt or dz]
    s_z = {(dt, dz): Copy("s_z", sq_block(dn(tok, dt), x, dn(zl, dz), y)) for dt, dz in turns}
    s_x = {d: Copy("s_x", sq_chunk(dn(x, d), y)) for d in SIDES}
    s_xf = [Copy("s_xf", sq_chunk(up(x, 2), y, 128 * i, 128)) for i in range(2)]
    s_y = {(j, d): Copy("s_y", sq_chunk(dn(x, j), dn(y, d))) for j in range(4) for d in SIDES}
    s_f = {j: Copy("s_f", sq_chunk(dn(x, j), up(y, 2))) for j in range(4)}
    u_y = {d: Copy("u_y", sq_rest(x, dn(y, d))) for d in THREE}
    u_x = {(j, d): Copy("u_x", sq_rest(dn(x, d), dn(y, j))) for j in range(4) for d in SIDES}
    u_f = {j: Copy("u_f", sq_rest(up(x, 2), dn(y, j))) for j in range(4)}

    def sg_at(t, h):
        return sg.at[:, rows_of(h), lanes(t)]

    t_far = [Copy("t_far", sg_at(far, h)) for h in parts]
    t_sib = [Copy("t_sib", sg_at(sib, h)) for h in parts]
    t_both = [Copy("t_both", sg_at(up(sib, 2), h)) for h in parts]

    def all_of(*groups):
        for group in groups:
            for copy in group.values() if isinstance(group, dict) else group:
                copy.arrived()

    for d in THREE:
        a_z[d].start(acts, xa_at(x, zl), dev(zl=up(zl, d)))
    for d in SIDES:
        a_x[0, d].start(acts, xa_at(x, zl), dev(x=up(x, d)))
    for d in THREE:
        b_a[d].start(basis_a.at[pl.ds(pl.multiple_of(c * (da // 2), da // 2), da // 2), ba_cols(up(y, d))], ba_at(y, c),
                     dev(y=up(y, d)))
    for d in SIDES:
        g_y[0, d].start(main, xg_at(y, zl), dev(y=up(y, d)))
    for d in THREE:
        v_y[d].start(rest, xv_at(y, zl), dev(y=up(y, d)))
    own_a = [local(acts, xa_at(x, zl)), local(basis_a.at[:, ba_cols(y)], ba.at[pl.ds(pl.multiple_of(y * da, da), da), :])]
    own_g = [local(grads, xg.at[y, pl.ds(pl.multiple_of(zl * dg, 32), dg), :])]
    own_g += [local(bg_cols(h, ys, x), bg_at(h, ys, x)) for h in parts for ys in mine + theirs]
    own_s = []

    def ax(j):
        a_z[j].arrived()
        for d in SIDES:
            a_x[j, d].start(xa_at(x, dn(zl, j)), xa_at(x, dn(zl, j)), dev(x=up(x, d)))

    def af(j):
        d = way(j)
        a_x[j, d].arrived()
        a_f[j].start(xa_at(dn(x, d), dn(zl, j)), xa_at(dn(x, d), dn(zl, j)), dev(x=up(x, d)))

    def share_a(d):
        b_a[d].arrived()
        a_s[d].start(ba_at(dn(y, d), c), ba_at(dn(y, d), c), dev(tok=sib))

    def project_a():
        for cp in own_a:
            cp.wait()
        all_of(a_x, a_f, b_a, a_s)
        for ys in range(NY):
            pa[ys] = jnp.dot(ba[...], xa[:, ys * quarter:(ys + 1) * quarter], preferred_element_type=F32)
        for d in THREE:
            p_a[d].start(pa.at[up(y, d)], ra.at[d - 1], dev(y=up(y, d)))

    def square_a():
        all_of(p_a)
        total = pa[y] + ra[0] + ra[1] + ra[2]
        sa[...] = (total * total).astype(BF16)
        for dt, dz in turns:
            t = up(tok, dt)
            s_z[dt, dz].start(sa.at[pl.ds(pl.multiple_of(t * da, da), da), :], sq_block(tok, x, zl, y),
                              dev(tok=t, zl=up(zl, dz)))
        own_s.append(local(sa.at[pl.ds(pl.multiple_of(tok * da, da), da), :], sq_block(tok, x, zl, y)))

    def spread(j):
        for d in SIDES:
            s_y[j, d].start(sq_chunk(dn(x, j), y), sq_chunk(dn(x, j), y), dev(y=up(y, d)))

    def spread_rest(j):
        for d in SIDES:
            u_x[j, d].start(sq_rest(x, dn(y, j)), sq_rest(x, dn(y, j)), dev(x=up(x, d)))

    def sx():
        own_s[0].wait()
        all_of(s_z)
        for d in SIDES:
            s_x[d].start(sq_chunk(x, y), sq_chunk(x, y), dev(x=up(x, d)))
        spread(0)
        for d in THREE:
            u_y[d].start(sq_rest(x, y), sq_rest(x, y), dev(y=up(y, d)))
        spread_rest(0)

    def sxf(i):
        d = SIDES[i]
        s_x[d].arrived()
        part = sq_chunk(dn(x, d), y, 128 * i, 128)
        s_xf[i].start(part, part, dev(x=up(x, d)))

    def ss(j):
        all_of(s_xf if j == 2 else [s_x[j]])
        spread(j)

    def sf(j):
        d = way(j)
        s_y[j, d].arrived()
        s_f[j].start(sq_chunk(dn(x, j), dn(y, d)), sq_chunk(dn(x, j), dn(y, d)), dev(y=up(y, d)))

    def us(j):
        u_y[j].arrived()
        spread_rest(j)

    def uf(j):
        d = way(j)
        u_x[j, d].arrived()
        u_f[j].start(sq_rest(dn(x, d), dn(y, j)), sq_rest(dn(x, d), dn(y, j)), dev(x=up(x, d)))

    def gz(d):
        g_z[d].start(main, xg_at(y, zl), dev(zl=up(zl, d)))

    def gs(j):
        g_z[j].arrived()
        for d in SIDES:
            g_y[j, d].start(xg_at(y, dn(zl, j)), xg_at(y, dn(zl, j)), dev(y=up(y, d)))

    def gf(j):
        d = way(j)
        g_y[j, d].arrived()
        g_f[j].start(xg_at(dn(y, d), dn(zl, j)), xg_at(dn(y, d), dn(zl, j)), dev(y=up(y, d)))

    def vz(i):
        if i:
            v_y[i].arrived()
        for d in THREE:
            v_z[i, d].start(xv_at(dn(y, i), zl) if i else rest, xv_at(dn(y, i), zl), dev(zl=up(zl, d)))

    def bx(h, k, d):
        b_x[h, k, d].start(bg_cols(h, mine[k], up(x, d)), bg_at(h, mine[k], x), dev(x=up(x, d)))

    def bs(h, k, d):
        b_x[h, k, d].arrived()
        b_s[h, k, d].start(bg_at(h, mine[k], dn(x, d)), bg_at(h, mine[k], dn(x, d)), dev(tok=sib))

    def cg(h, i):
        while own_g:
            own_g.pop().wait()
        for d in THREE:
            all_of([b_x[h, i // 2, d], b_s[h, i // 2, d]])
        ring = (0, 1, 3, 2)[i]
        if i == 0:
            all_of(g_z)
        elif i == 3:
            all_of(g_f)
        else:
            all_of([g_y[j, ring] for j in range(4)])
        all_of([v_z[ring, d] for d in THREE], [v_y[ring]] if ring else [])
        ys = dn(y, ring)
        rows = slice(NX * at[h], NX * (at[h] + PARTS[h]))
        part = jnp.dot(bg[ys, rows, :], xg[ys], preferred_element_type=F32)
        acc[rows, :] = part if i == 0 else acc[rows, :] + part
        if i == 3:
            ps[rows, :] = acc[rows, :].astype(BF16)
            for d in (2, 1, 3):
                xs = up(x, d)
                p_g[h, d].start(ps.at[part_rows(h, xs), :], pr.at[d - 1, rows_of(h), :], dev(x=xs))

    def square_g(h):
        all_of([p_g[h, d] for d in THREE])
        total = acc[part_rows(h, x), :]
        for d in range(NX - 1):
            total = total + pr[d, rows_of(h), :].astype(F32)
        square = (total * total).astype(BF16)
        for q in range(NY):
            sg[q, rows_of(h), lanes(tok)] = square[:, q * quarter:(q + 1) * quarter]
        t_far[h].start(sg_at(tok, h), sg_at(tok, h), dev(tok=far))
        t_sib[h].start(sg_at(tok, h), sg_at(tok, h), dev(tok=sib))

    def tb(h):
        t_far[h].arrived()
        t_both[h].start(sg_at(far, h), sg_at(far, h), dev(tok=sib))

    def fin(i):
        all_of(*((s_x, s_xf, s_y, s_f, u_y, u_x, u_f), (t_sib,), (t_far,), (t_both,))[i])
        if i < 3:
            return
        left = jnp.concatenate([sg[q] for q in range(NY)], axis=1)
        tile = 256
        for n in range(0, out.shape[1], tile):
            right = jnp.concatenate([sq[q, n:n + tile, :] for q in range(NY)], axis=1)
            value = lax.dot_general(left, right, (((1,), (1,)), ((), ())), preferred_element_type=F32)
            out[:, n:n + tile] = value * (1.0 / (cols * NT))

    steps = {"ax": ax, "af": af, "as": share_a, "pa": project_a, "sa": square_a, "sx": sx, "sxf": sxf, "ss": ss, "sf": sf,
             "us": us, "uf": uf, "gz": gz, "gs": gs, "gf": gf, "vz": vz, "bx": bx, "bs": bs, "cg": cg, "sq": square_g, "tb": tb,
             "fin": fin}
    for name, *where in SCHEDULE:
        steps[name](*where)

    for cp in sent:
        cp.wait_send()


def body(acts_t, grads_t, basis_a, basis_g):
    da, cols = acts_t.shape
    dg = grads_t.shape[0]
    fa = basis_a.shape[1] // NY
    rows_a, quarter = NY * da, cols // NY
    fx = NZ * dg
    anywhere = pl.BlockSpec(memory_space=pl.ANY)
    n_out = basis_a.shape[1] // NT
    return pl.pallas_call(
        kernel,
        out_shape=jax.ShapeDtypeStruct((dg, n_out), F32),
        in_specs=[anywhere] * 4,
        out_specs=pl.BlockSpec(memory_space=pltpu.VMEM),
        scratch_shapes=[
            pltpu.VMEM((fa, cols), BF16),
            pltpu.VMEM((rows_a, fa), BF16),
            pltpu.VMEM((NY, rows_a, quarter), F32),
            pltpu.VMEM((NY - 1, rows_a, quarter), F32),
            pltpu.VMEM((rows_a, quarter), BF16),
            pltpu.VMEM((NY, n_out, NT * quarter), BF16),
            pltpu.VMEM((NY, fx, cols), BF16),
            pltpu.VMEM((NY, NX * dg, fx), BF16),
            pltpu.VMEM((NX * dg, cols), F32),
            pltpu.VMEM((NX * dg, cols), BF16),
            pltpu.VMEM((NX - 1, dg, cols), BF16),
            pltpu.VMEM((NY, dg, NT * quarter), BF16),
            pltpu.SemaphoreType.DMA((N_COPIES,)),
            pltpu.SemaphoreType.DMA((N_COPIES,)),
            pltpu.SemaphoreType.DMA((N_LOCAL,)),
        ],
        compiler_params=pltpu.CompilerParams(
            collective_id=0, has_side_effects=True, vmem_limit_bytes=60 * 2**20
        ),
    )(acts_t, grads_t, basis_a, basis_g)


def solution(mesh):
    return jax.shard_map(
        body,
        mesh=mesh,
        in_specs=(P("col", "tok"), P("col", "tok"), P("col", None), P("col", None)),
        out_specs=P("col", "tok"),
        check_vma=False,
    )
```

```python
import jax
import jax.numpy as jnp
from jax import lax
from jax.experimental import pallas as pl
from jax.experimental.pallas import tpu as pltpu
from jax.sharding import PartitionSpec as P

MESH = pl.DeviceIdType.MESH
BF16 = jnp.bfloat16
F32 = jnp.float32
NX, NY, NZ, NT = 4, 4, 4, 4


class Sems:
    def __init__(self, send, recv):
        self.send, self.recv, self.used = send, recv, 0

    def take(self):
        i = self.used
        self.used += 1
        return self.send.at[i], self.recv.at[i]


N_COPIES = 144
N_LOCAL = 24

THREE = (1, 3, 2)
SIDES = (1, 3)


def way(j):
    return 1 if j < 2 else 3


SCHEDULE = (
    ("bx", 0, 0, 2), ("ax", 1), ("gz", 2), ("ax", 3), ("gf", 0), ("ax", 2), ("af", 0), ("af", 3), ("af", 1),
    ("as", 3), ("af", 2), ("vz", 0), ("gs", 2), ("as", 2), ("bx", 0, 0, 1), ("gz", 1), ("bx", 0, 0, 3),
    ("bx", 1, 0, 1), ("bs", 0, 0, 2), ("as", 1), ("pa",), ("bx", 1, 0, 3), ("gf", 2), ("gz", 3), ("bx", 0, 1, 1),
    ("bx", 0, 1, 3), ("gs", 1), ("bs", 0, 0, 1), ("bx", 1, 1, 2), ("sa",), ("gs", 3), ("bx", 0, 1, 2),
    ("bs", 0, 0, 3), ("bs", 0, 1, 3), ("sx",), ("bs", 0, 1, 1), ("vz", 3), ("vz", 1), ("bs", 0, 1, 2), ("gf", 3),
    ("gf", 1), ("bx", 1, 0, 2), ("cg", 0, 0), ("vz", 2), ("sxf", 1), ("sxf", 0), ("bs", 1, 1, 2), ("bx", 1, 1, 3),
    ("bs", 1, 0, 3), ("bs", 1, 0, 1), ("cg", 0, 1), ("ss", 3), ("bx", 1, 1, 1), ("cg", 0, 2), ("cg", 0, 3),
    ("bs", 1, 0, 2), ("ss", 2), ("bs", 1, 1, 1), ("ss", 1), ("cg", 1, 0), ("sf", 3), ("cg", 1, 1), ("bs", 1, 1, 3),
    ("cg", 1, 2), ("us", 2), ("sf", 0), ("us", 1), ("cg", 1, 3), ("us", 3), ("sq", 0), ("sf", 2), ("sf", 1),
    ("uf", 1), ("uf", 2), ("sq", 1), ("uf", 3), ("uf", 0), ("tb", 0), ("fin", 0), ("tb", 1), ("fin", 1), ("fin", 2),
    ("fin", 3),
)


SPLIT = 3
PARTS = (160, 64)
FLIP = 32


def kernel(acts, grads, basis_a, basis_g, out, xa, ba, pa, ra, sa, sq, xg, bg, acc, ps, pr, sg,
           send_sem, recv_sem, local_sem):
    tok = lax.axis_index("tok")
    col = lax.axis_index("col")
    zl = lax.rem(col, 4)
    x = lax.rem(lax.div(col, 4), 4)
    y = lax.div(col, 16)
    c = lax.rem(tok, 2)
    da, fa = acts.shape[0], basis_a.shape[1] // NY
    dg = grads.shape[0]
    at = [sum(PARTS[:h]) for h in range(len(PARTS))]
    flip = FLIP
    fx = NZ * dg
    fy = NX * fx
    cols = acts.shape[1]
    quarter = cols // NY

    def up(v, d):
        return lax.rem(v + d, 4)

    def dn(v, d):
        return lax.rem(v + 4 - d, 4)

    def dev(tok=tok, y=y, x=x, zl=zl):
        return (tok, (y * 4 + x) * 4 + zl)

    sib = tok + 1 - 2 * c
    far = up(tok, 2)

    barrier = pltpu.get_barrier_semaphore()
    partners = [dev(tok=up(tok, dt), zl=up(zl, dz)) for dt in range(4) for dz in range(4) if dt or dz]
    partners += [dev(x=up(x, d)) for d in (1, 2, 3)] + [dev(y=up(y, d)) for d in (1, 2, 3)]
    for p in partners:
        pl.semaphore_signal(barrier, inc=1, device_id=p, device_id_type=MESH)
    pl.semaphore_wait(barrier, len(partners))

    sems = Sems(send_sem, recv_sem)
    sent = []

    class Copy:
        def __init__(self, tag, landing):
            self.tag, self.landing, self.sems, self.here = tag, landing, sems.take(), False

        def start(self, src, dst, to):
            s, r = self.sems
            cp = pltpu.make_async_remote_copy(src_ref=src, dst_ref=dst, send_sem=s, recv_sem=r,
                                              device_id=to, device_id_type=MESH)
            cp.start()
            sent.append((self.tag, cp))

        def arrived(self):
            if self.here:
                return
            self.here = True
            s, r = self.sems
            pltpu.make_async_remote_copy(src_ref=self.landing, dst_ref=self.landing, send_sem=s, recv_sem=r,
                                         device_id=dev(), device_id_type=MESH).wait_recv()

    n_local = [0]

    def local(src, dst):
        cp = pltpu.make_async_copy(src, dst, local_sem.at[n_local[0]])
        n_local[0] += 1
        cp.start()
        return cp

    def xa_at(xs, zs):
        return xa.at[pl.ds(pl.multiple_of(xs * (NZ * da) + zs * da, da), da), :]

    def ba_at(ys, core):
        return ba.at[pl.ds(pl.multiple_of(ys * da + core * (da // 2), da // 2), da // 2), :]

    def ba_cols(ys):
        return pl.ds(pl.multiple_of(ys * fa, fa), fa)

    def xg_at(ys, zs):
        return xg.at[ys, pl.ds(pl.multiple_of(zs * dg, 32), dg - flip), :]

    def xv_at(ys, zs):
        return xg.at[ys, pl.ds(pl.multiple_of(zs * dg + (dg - flip), 32), flip), :]

    def bg_at(h, ys, xs):
        return bg.at[ys, pl.ds(pl.multiple_of(NX * at[h] + xs * PARTS[h], 16), PARTS[h]), :]

    def bg_cols(h, ys, xs):
        return basis_g.at[at[h]:at[h] + PARTS[h], pl.ds(pl.multiple_of(ys * fy + xs * fx, 128), fx)]

    def part_rows(h, xs):
        return pl.ds(pl.multiple_of(NX * at[h] + xs * PARTS[h], 16), PARTS[h])

    def rows_of(h):
        return pl.ds(at[h], PARTS[h])

    parts = range(len(PARTS))
    main, rest = grads.at[0:dg - flip, :], grads.at[dg - flip:dg, :]

    def lanes(q):
        return pl.ds(pl.multiple_of(q * quarter, quarter), quarter)

    def sq_block(t, xs, zs, q):
        return sq.at[t, pl.ds(pl.multiple_of((xs * NZ + zs) * da, da), da), lanes(q)]

    def sq_chunk(xs, q, first=0, rows=NZ * da):
        return sq.at[0:SPLIT, pl.ds(pl.multiple_of(xs * (NZ * da) + first, 128), rows), lanes(q)]

    def sq_rest(xs, q):
        return sq.at[SPLIT:NT, pl.ds(pl.multiple_of(xs * (NZ * da), NZ * da), NZ * da), lanes(q)]

    a_z = {d: Copy("a_z", xa_at(x, dn(zl, d))) for d in THREE}
    a_x = {(j, d): Copy("a_x", xa_at(dn(x, d), dn(zl, j))) for j in range(4) for d in SIDES}
    a_f = {j: Copy("a_f", xa_at(up(x, 2), dn(zl, j))) for j in range(4)}
    b_a = {d: Copy("b_a", ba_at(dn(y, d), c)) for d in THREE}
    a_s = {d: Copy("a_s", ba_at(dn(y, d), 1 - c)) for d in THREE}
    p_a = {d: Copy("p_a", ra.at[d - 1]) for d in THREE}
    g_z = {d: Copy("g_z", xg_at(y, dn(zl, d))) for d in THREE}
    g_y = {(j, d): Copy("g_y", xg_at(dn(y, d), dn(zl, j))) for j in range(4) for d in SIDES}
    g_f = {j: Copy("g_f", xg_at(up(y, 2), dn(zl, j))) for j in range(4)}
    v_y = {d: Copy("v_y", xv_at(dn(y, d), zl)) for d in THREE}
    v_z = {(i, d): Copy("v_z", xv_at(dn(y, i), dn(zl, d))) for i in range(4) for d in THREE}
    mine = [up(y, 3 * c), up(y, 1 + c)]
    theirs = [up(y, 3 * (1 - c)), up(y, 2 - c)]
    pieces = [(h, k, d) for h in parts for k in range(2) for d in THREE]
    b_x = {(h, k, d): Copy("b_x", bg_at(h, mine[k], dn(x, d))) for h, k, d in pieces}
    b_s = {(h, k, d): Copy("b_s", bg_at(h, theirs[k], dn(x, d))) for h, k, d in pieces}
    p_g = {(h, d): Copy("p_g", pr.at[d - 1, rows_of(h), :]) for h in parts for d in THREE}
    turns = [(dt, dz) for dt in range(4) for dz in range(4) if dt or dz]
    s_z = {(dt, dz): Copy("s_z", sq_block(dn(tok, dt), x, dn(zl, dz), y)) for dt, dz in turns}
    s_x = {d: Copy("s_x", sq_chunk(dn(x, d), y)) for d in SIDES}
    s_xf = [Copy("s_xf", sq_chunk(up(x, 2), y, 128 * i, 128)) for i in range(2)]
    s_y = {(j, d): Copy("s_y", sq_chunk(dn(x, j), dn(y, d))) for j in range(4) for d in SIDES}
    s_f = {j: Copy("s_f", sq_chunk(dn(x, j), up(y, 2))) for j in range(4)}
    u_y = {d: Copy("u_y", sq_rest(x, dn(y, d))) for d in THREE}
    u_x = {(j, d): Copy("u_x", sq_rest(dn(x, d), dn(y, j))) for j in range(4) for d in SIDES}
    u_f = {j: Copy("u_f", sq_rest(up(x, 2), dn(y, j))) for j in range(4)}

    def sg_at(t, h):
        return sg.at[t, rows_of(h), :]

    t_far = [Copy("t_far", sg_at(far, h)) for h in parts]
    t_sib = [Copy("t_sib", sg_at(sib, h)) for h in parts]
    t_both = [Copy("t_both", sg_at(up(sib, 2), h)) for h in parts]

    def all_of(*groups):
        for group in groups:
            for copy in group.values() if isinstance(group, dict) else group:
                copy.arrived()

    for d in THREE:
        a_z[d].start(acts, xa_at(x, zl), dev(zl=up(zl, d)))
    for d in SIDES:
        a_x[0, d].start(acts, xa_at(x, zl), dev(x=up(x, d)))
    for d in THREE:
        b_a[d].start(basis_a.at[pl.ds(pl.multiple_of(c * (da // 2), da // 2), da // 2), ba_cols(up(y, d))], ba_at(y, c),
                     dev(y=up(y, d)))
    for d in SIDES:
        g_y[0, d].start(main, xg_at(y, zl), dev(y=up(y, d)))
    for d in THREE:
        v_y[d].start(rest, xv_at(y, zl), dev(y=up(y, d)))
    own_a = [local(acts, xa_at(x, zl)), local(basis_a.at[:, ba_cols(y)], ba.at[pl.ds(pl.multiple_of(y * da, da), da), :])]
    own_g = [local(grads, xg.at[y, pl.ds(pl.multiple_of(zl * dg, 32), dg), :])]
    own_g += [local(bg_cols(h, ys, x), bg_at(h, ys, x)) for h in parts for ys in mine + theirs]
    own_s = []

    def ax(j):
        a_z[j].arrived()
        for d in SIDES:
            a_x[j, d].start(xa_at(x, dn(zl, j)), xa_at(x, dn(zl, j)), dev(x=up(x, d)))

    def af(j):
        d = way(j)
        a_x[j, d].arrived()
        a_f[j].start(xa_at(dn(x, d), dn(zl, j)), xa_at(dn(x, d), dn(zl, j)), dev(x=up(x, d)))

    def share_a(d):
        b_a[d].arrived()
        a_s[d].start(ba_at(dn(y, d), c), ba_at(dn(y, d), c), dev(tok=sib))

    def project_a():
        for cp in own_a:
            cp.wait()
        all_of(a_x, a_f, b_a, a_s)
        for ys in range(NY):
            pa[ys] = jnp.dot(ba[...], xa[:, ys * quarter:(ys + 1) * quarter], preferred_element_type=F32)
        for d in THREE:
            p_a[d].start(pa.at[up(y, d)], ra.at[d - 1], dev(y=up(y, d)))

    def square_a():
        all_of(p_a)
        total = pa[y] + ra[0] + ra[1] + ra[2]
        sa[...] = (total * total).astype(BF16)
        for dt, dz in turns:
            t = up(tok, dt)
            s_z[dt, dz].start(sa.at[pl.ds(pl.multiple_of(t * da, da), da), :], sq_block(tok, x, zl, y),
                              dev(tok=t, zl=up(zl, dz)))
        own_s.append(local(sa.at[pl.ds(pl.multiple_of(tok * da, da), da), :], sq_block(tok, x, zl, y)))

    def spread(j):
        for d in SIDES:
            s_y[j, d].start(sq_chunk(dn(x, j), y), sq_chunk(dn(x, j), y), dev(y=up(y, d)))

    def spread_rest(j):
        for d in SIDES:
            u_x[j, d].start(sq_rest(x, dn(y, j)), sq_rest(x, dn(y, j)), dev(x=up(x, d)))

    def sx():
        own_s[0].wait()
        all_of(s_z)
        for d in SIDES:
            s_x[d].start(sq_chunk(x, y), sq_chunk(x, y), dev(x=up(x, d)))
        spread(0)
        for d in THREE:
            u_y[d].start(sq_rest(x, y), sq_rest(x, y), dev(y=up(y, d)))
        spread_rest(0)

    def sxf(i):
        d = SIDES[i]
        s_x[d].arrived()
        part = sq_chunk(dn(x, d), y, 128 * i, 128)
        s_xf[i].start(part, part, dev(x=up(x, d)))

    def ss(j):
        all_of(s_xf if j == 2 else [s_x[j]])
        spread(j)

    def sf(j):
        d = way(j)
        s_y[j, d].arrived()
        s_f[j].start(sq_chunk(dn(x, j), dn(y, d)), sq_chunk(dn(x, j), dn(y, d)), dev(y=up(y, d)))

    def us(j):
        u_y[j].arrived()
        spread_rest(j)

    def uf(j):
        d = way(j)
        u_x[j, d].arrived()
        u_f[j].start(sq_rest(dn(x, d), dn(y, j)), sq_rest(dn(x, d), dn(y, j)), dev(x=up(x, d)))

    def gz(d):
        g_z[d].start(main, xg_at(y, zl), dev(zl=up(zl, d)))

    def gs(j):
        g_z[j].arrived()
        for d in SIDES:
            g_y[j, d].start(xg_at(y, dn(zl, j)), xg_at(y, dn(zl, j)), dev(y=up(y, d)))

    def gf(j):
        d = way(j)
        g_y[j, d].arrived()
        g_f[j].start(xg_at(dn(y, d), dn(zl, j)), xg_at(dn(y, d), dn(zl, j)), dev(y=up(y, d)))

    def vz(i):
        if i:
            v_y[i].arrived()
        for d in THREE:
            v_z[i, d].start(xv_at(dn(y, i), zl) if i else rest, xv_at(dn(y, i), zl), dev(zl=up(zl, d)))

    def bx(h, k, d):
        b_x[h, k, d].start(bg_cols(h, mine[k], up(x, d)), bg_at(h, mine[k], x), dev(x=up(x, d)))

    def bs(h, k, d):
        b_x[h, k, d].arrived()
        b_s[h, k, d].start(bg_at(h, mine[k], dn(x, d)), bg_at(h, mine[k], dn(x, d)), dev(tok=sib))

    def cg(h, i):
        while own_g:
            own_g.pop().wait()
        for d in THREE:
            all_of([b_x[h, i // 2, d], b_s[h, i // 2, d]])
        ring = (0, 1, 3, 2)[i]
        if i == 0:
            all_of(g_z)
        elif i == 3:
            all_of(g_f)
        else:
            all_of([g_y[j, ring] for j in range(4)])
        all_of([v_z[ring, d] for d in THREE], [v_y[ring]] if ring else [])
        ys = dn(y, ring)
        rows = slice(NX * at[h], NX * (at[h] + PARTS[h]))
        part = jnp.dot(bg[ys, rows, :], xg[ys], preferred_element_type=F32)
        acc[rows, :] = part if i == 0 else acc[rows, :] + part
        if i == 3:
            ps[rows, :] = acc[rows, :].astype(BF16)
            for d in (2, 1, 3):
                xs = up(x, d)
                p_g[h, d].start(ps.at[part_rows(h, xs), :], pr.at[d - 1, rows_of(h), :], dev(x=xs))

    def square_g(h):
        all_of([p_g[h, d] for d in THREE])
        total = acc[part_rows(h, x), :]
        for d in range(NX - 1):
            total = total + pr[d, rows_of(h), :].astype(F32)
        sg[tok, rows_of(h), :] = (total * total).astype(BF16)
        t_far[h].start(sg_at(tok, h), sg_at(tok, h), dev(tok=far))
        t_sib[h].start(sg_at(tok, h), sg_at(tok, h), dev(tok=sib))

    def tb(h):
        t_far[h].arrived()
        t_both[h].start(sg_at(far, h), sg_at(far, h), dev(tok=sib))

    tile = 256
    scale = 1.0 / (cols * NT)

    def settle(recent):
        for tag, cp in [one for one in sent if one[0] not in recent]:
            cp.wait_send()
            sent.remove((tag, cp))

    def fin(i):
        if i == 0:
            settle(("s_y", "s_f", "u_x", "u_f", "t_far", "t_sib", "t_both"))
        all_of(*((s_x, s_xf, s_y, s_f, u_y, u_x, u_f), (t_sib,), (t_far,), (t_both,))[i])
        t = (tok, sib, far, up(sib, 2))[i]
        for n in range(0, out.shape[1], tile):
            part = lax.dot_general(sg[t], sq[t, n:n + tile, :], (((1,), (1,)), ((), ())), preferred_element_type=F32)
            value = part if i == 0 else out[:, n:n + tile] + part
            out[:, n:n + tile] = value * scale if i == 3 else value

    steps = {"ax": ax, "af": af, "as": share_a, "pa": project_a, "sa": square_a, "sx": sx, "sxf": sxf, "ss": ss, "sf": sf,
             "us": us, "uf": uf, "gz": gz, "gs": gs, "gf": gf, "vz": vz, "bx": bx, "bs": bs, "cg": cg, "sq": square_g, "tb": tb,
             "fin": fin}
    for name, *where in SCHEDULE:
        steps[name](*where)

    settle(())


def body(acts_t, grads_t, basis_a, basis_g):
    da, cols = acts_t.shape
    dg = grads_t.shape[0]
    fa = basis_a.shape[1] // NY
    rows_a, quarter = NY * da, cols // NY
    fx = NZ * dg
    anywhere = pl.BlockSpec(memory_space=pl.ANY)
    n_out = basis_a.shape[1] // NT
    return pl.pallas_call(
        kernel,
        out_shape=jax.ShapeDtypeStruct((dg, n_out), F32),
        in_specs=[anywhere] * 4,
        out_specs=pl.BlockSpec(memory_space=pltpu.VMEM),
        scratch_shapes=[
            pltpu.VMEM((fa, cols), BF16),
            pltpu.VMEM((rows_a, fa), BF16),
            pltpu.VMEM((NY, rows_a, quarter), F32),
            pltpu.VMEM((NY - 1, rows_a, quarter), F32),
            pltpu.VMEM((rows_a, quarter), BF16),
            pltpu.VMEM((NT, n_out, cols), BF16),
            pltpu.VMEM((NY, fx, cols), BF16),
            pltpu.VMEM((NY, NX * dg, fx), BF16),
            pltpu.VMEM((NX * dg, cols), F32),
            pltpu.VMEM((NX * dg, cols), BF16),
            pltpu.VMEM((NX - 1, dg, cols), BF16),
            pltpu.VMEM((NT, dg, cols), BF16),
            pltpu.SemaphoreType.DMA((N_COPIES,)),
            pltpu.SemaphoreType.DMA((N_COPIES,)),
            pltpu.SemaphoreType.DMA((N_LOCAL,)),
        ],
        compiler_params=pltpu.CompilerParams(
            collective_id=0, has_side_effects=True, vmem_limit_bytes=60 * 2**20
        ),
    )(acts_t, grads_t, basis_a, basis_g)


def solution(mesh):
    return jax.shard_map(
        body,
        mesh=mesh,
        in_specs=(P("col", "tok"), P("col", "tok"), P("col", None), P("col", None)),
        out_specs=P("col", "tok"),
        check_vma=False,
    )
```

```python
import jax
import jax.numpy as jnp
from jax import lax
from jax.experimental import pallas as pl
from jax.experimental.pallas import tpu as pltpu
from jax.sharding import PartitionSpec as P

MESH = pl.DeviceIdType.MESH
BF16 = jnp.bfloat16
F32 = jnp.float32
NX, NY, NZ, NT = 4, 4, 4, 4


class Sems:
    def __init__(self, send, recv):
        self.send, self.recv, self.used = send, recv, 0

    def take(self):
        i = self.used
        self.used += 1
        return self.send.at[i], self.recv.at[i]


N_COPIES = 144
N_LOCAL = 24

THREE = (1, 3, 2)
SIDES = (1, 3)


def way(j):
    return 1 if j < 2 else 3


SCHEDULE = (
    ("bx", 0, 0, 2), ("ax", 1), ("gz", 2), ("ax", 3), ("gf", 0), ("ax", 2), ("af", 0), ("af", 3), ("af", 1),
    ("as", 3), ("af", 2), ("vz", 0), ("gs", 2), ("as", 2), ("bx", 0, 0, 1), ("gz", 1), ("bx", 0, 0, 3),
    ("bx", 1, 0, 1), ("bs", 0, 0, 2), ("as", 1), ("pa",), ("bx", 1, 0, 3), ("gf", 2), ("gz", 3), ("bx", 0, 1, 1),
    ("bx", 0, 1, 3), ("gs", 1), ("bs", 0, 0, 1), ("bx", 1, 1, 2), ("sa",), ("gs", 3), ("bx", 0, 1, 2),
    ("bs", 0, 0, 3), ("bs", 0, 1, 3), ("sx",), ("bs", 0, 1, 1), ("vz", 3), ("vz", 1), ("bs", 0, 1, 2), ("gf", 3),
    ("gf", 1), ("bx", 1, 0, 2), ("cg", 0, 0), ("vz", 2), ("sxf", 1), ("sxf", 0), ("bs", 1, 1, 2), ("bx", 1, 1, 3),
    ("bs", 1, 0, 3), ("bs", 1, 0, 1), ("cg", 0, 1), ("ss", 3), ("bx", 1, 1, 1), ("cg", 0, 2), ("cg", 0, 3),
    ("bs", 1, 0, 2), ("ss", 2), ("bs", 1, 1, 1), ("ss", 1), ("cg", 1, 0), ("sf", 3), ("cg", 1, 1), ("bs", 1, 1, 3),
    ("cg", 1, 2), ("us", 2), ("sf", 0), ("us", 1), ("cg", 1, 3), ("us", 3), ("sq", 0), ("sf", 2), ("sf", 1),
    ("uf", 1), ("uf", 2), ("sq", 1), ("uf", 3), ("uf", 0), ("tb", 0), ("fin", 0), ("tb", 1), ("fin", 1), ("fin", 2),
    ("fin", 3),
)


SPLIT = 3
PARTS = (144, 80)
FLIP = 32


def kernel(acts, grads, basis_a, basis_g, out, xa, ba, pa, ra, sa, sq, xg, bg, acc, ps, pr, sg,
           send_sem, recv_sem, local_sem):
    tok = lax.axis_index("tok")
    col = lax.axis_index("col")
    zl = lax.rem(col, 4)
    x = lax.rem(lax.div(col, 4), 4)
    y = lax.div(col, 16)
    c = lax.rem(tok, 2)
    da, fa = acts.shape[0], basis_a.shape[1] // NY
    dg = grads.shape[0]
    at = [sum(PARTS[:h]) for h in range(len(PARTS))]
    flip = FLIP
    fx = NZ * dg
    fy = NX * fx
    cols = acts.shape[1]
    quarter = cols // NY

    def up(v, d):
        return lax.rem(v + d, 4)

    def dn(v, d):
        return lax.rem(v + 4 - d, 4)

    def dev(tok=tok, y=y, x=x, zl=zl):
        return (tok, (y * 4 + x) * 4 + zl)

    sib = tok + 1 - 2 * c
    far = up(tok, 2)

    barrier = pltpu.get_barrier_semaphore()
    partners = [dev(tok=up(tok, dt), zl=up(zl, dz)) for dt in range(4) for dz in range(4) if dt or dz]
    partners += [dev(x=up(x, d)) for d in (1, 2, 3)] + [dev(y=up(y, d)) for d in (1, 2, 3)]
    for p in partners:
        pl.semaphore_signal(barrier, inc=1, device_id=p, device_id_type=MESH)
    pl.semaphore_wait(barrier, len(partners))

    sems = Sems(send_sem, recv_sem)
    sent = []

    class Copy:
        def __init__(self, tag, landing):
            self.tag, self.landing, self.sems, self.here = tag, landing, sems.take(), False

        def start(self, src, dst, to):
            s, r = self.sems
            cp = pltpu.make_async_remote_copy(src_ref=src, dst_ref=dst, send_sem=s, recv_sem=r,
                                              device_id=to, device_id_type=MESH)
            cp.start()
            sent.append((self.tag, cp))

        def arrived(self):
            if self.here:
                return
            self.here = True
            s, r = self.sems
            pltpu.make_async_remote_copy(src_ref=self.landing, dst_ref=self.landing, send_sem=s, recv_sem=r,
                                         device_id=dev(), device_id_type=MESH).wait_recv()

    n_local = [0]

    def local(src, dst):
        cp = pltpu.make_async_copy(src, dst, local_sem.at[n_local[0]])
        n_local[0] += 1
        cp.start()
        return cp

    def xa_at(xs, zs):
        return xa.at[pl.ds(pl.multiple_of(xs * (NZ * da) + zs * da, da), da), :]

    def ba_at(ys, core):
        return ba.at[pl.ds(pl.multiple_of(ys * da + core * (da // 2), da // 2), da // 2), :]

    def ba_cols(ys):
        return pl.ds(pl.multiple_of(ys * fa, fa), fa)

    def xg_at(ys, zs):
        return xg.at[ys, pl.ds(pl.multiple_of(zs * dg, 32), dg - flip), :]

    def xv_at(ys, zs):
        return xg.at[ys, pl.ds(pl.multiple_of(zs * dg + (dg - flip), 32), flip), :]

    def bg_at(h, ys, xs):
        return bg.at[ys, pl.ds(pl.multiple_of(NX * at[h] + xs * PARTS[h], 16), PARTS[h]), :]

    def bg_cols(h, ys, xs):
        return basis_g.at[at[h]:at[h] + PARTS[h], pl.ds(pl.multiple_of(ys * fy + xs * fx, 128), fx)]

    def part_rows(h, xs):
        return pl.ds(pl.multiple_of(NX * at[h] + xs * PARTS[h], 16), PARTS[h])

    def rows_of(h):
        return pl.ds(at[h], PARTS[h])

    parts = range(len(PARTS))
    main, rest = grads.at[0:dg - flip, :], grads.at[dg - flip:dg, :]

    def lanes(q):
        return pl.ds(pl.multiple_of(q * quarter, quarter), quarter)

    def sq_block(t, xs, zs, q):
        return sq.at[t, pl.ds(pl.multiple_of((xs * NZ + zs) * da, da), da), lanes(q)]

    def sq_chunk(xs, q, first=0, rows=NZ * da):
        return sq.at[0:SPLIT, pl.ds(pl.multiple_of(xs * (NZ * da) + first, 128), rows), lanes(q)]

    def sq_rest(xs, q):
        return sq.at[SPLIT:NT, pl.ds(pl.multiple_of(xs * (NZ * da), NZ * da), NZ * da), lanes(q)]

    a_z = {d: Copy("a_z", xa_at(x, dn(zl, d))) for d in THREE}
    a_x = {(j, d): Copy("a_x", xa_at(dn(x, d), dn(zl, j))) for j in range(4) for d in SIDES}
    a_f = {j: Copy("a_f", xa_at(up(x, 2), dn(zl, j))) for j in range(4)}
    b_a = {d: Copy("b_a", ba_at(dn(y, d), c)) for d in THREE}
    a_s = {d: Copy("a_s", ba_at(dn(y, d), 1 - c)) for d in THREE}
    p_a = {d: Copy("p_a", ra.at[d - 1]) for d in THREE}
    g_z = {d: Copy("g_z", xg_at(y, dn(zl, d))) for d in THREE}
    g_y = {(j, d): Copy("g_y", xg_at(dn(y, d), dn(zl, j))) for j in range(4) for d in SIDES}
    g_f = {j: Copy("g_f", xg_at(up(y, 2), dn(zl, j))) for j in range(4)}
    v_y = {d: Copy("v_y", xv_at(dn(y, d), zl)) for d in THREE}
    v_z = {(i, d): Copy("v_z", xv_at(dn(y, i), dn(zl, d))) for i in range(4) for d in THREE}
    mine = [up(y, 3 * c), up(y, 1 + c)]
    theirs = [up(y, 3 * (1 - c)), up(y, 2 - c)]
    pieces = [(h, k, d) for h in parts for k in range(2) for d in THREE]
    b_x = {(h, k, d): Copy("b_x", bg_at(h, mine[k], dn(x, d))) for h, k, d in pieces}
    b_s = {(h, k, d): Copy("b_s", bg_at(h, theirs[k], dn(x, d))) for h, k, d in pieces}
    p_g = {(h, d): Copy("p_g", pr.at[d - 1, rows_of(h), :]) for h in parts for d in THREE}
    turns = [(dt, dz) for dt in range(4) for dz in range(4) if dt or dz]
    s_z = {(dt, dz): Copy("s_z", sq_block(dn(tok, dt), x, dn(zl, dz), y)) for dt, dz in turns}
    s_x = {d: Copy("s_x", sq_chunk(dn(x, d), y)) for d in SIDES}
    s_xf = [Copy("s_xf", sq_chunk(up(x, 2), y, 128 * i, 128)) for i in range(2)]
    s_y = {(j, d): Copy("s_y", sq_chunk(dn(x, j), dn(y, d))) for j in range(4) for d in SIDES}
    s_f = {j: Copy("s_f", sq_chunk(dn(x, j), up(y, 2))) for j in range(4)}
    u_y = {d: Copy("u_y", sq_rest(x, dn(y, d))) for d in THREE}
    u_x = {(j, d): Copy("u_x", sq_rest(dn(x, d), dn(y, j))) for j in range(4) for d in SIDES}
    u_f = {j: Copy("u_f", sq_rest(up(x, 2), dn(y, j))) for j in range(4)}

    def sg_at(t, h):
        return sg.at[t, rows_of(h), :]

    t_far = [Copy("t_far", sg_at(far, h)) for h in parts]
    t_sib = [Copy("t_sib", sg_at(sib, h)) for h in parts]
    t_both = [Copy("t_both", sg_at(up(sib, 2), h)) for h in parts]

    def all_of(*groups):
        for group in groups:
            for copy in group.values() if isinstance(group, dict) else group:
                copy.arrived()

    for d in THREE:
        a_z[d].start(acts, xa_at(x, zl), dev(zl=up(zl, d)))
    for d in SIDES:
        a_x[0, d].start(acts, xa_at(x, zl), dev(x=up(x, d)))
    for d in THREE:
        b_a[d].start(basis_a.at[pl.ds(pl.multiple_of(c * (da // 2), da // 2), da // 2), ba_cols(up(y, d))], ba_at(y, c),
                     dev(y=up(y, d)))
    for d in SIDES:
        g_y[0, d].start(main, xg_at(y, zl), dev(y=up(y, d)))
    for d in THREE:
        v_y[d].start(rest, xv_at(y, zl), dev(y=up(y, d)))
    own_a = [local(acts, xa_at(x, zl)), local(basis_a.at[:, ba_cols(y)], ba.at[pl.ds(pl.multiple_of(y * da, da), da), :])]
    own_g = [local(grads, xg.at[y, pl.ds(pl.multiple_of(zl * dg, 32), dg), :])]
    own_g += [local(bg_cols(h, ys, x), bg_at(h, ys, x)) for h in parts for ys in mine + theirs]
    own_s = []

    def ax(j):
        a_z[j].arrived()
        for d in SIDES:
            a_x[j, d].start(xa_at(x, dn(zl, j)), xa_at(x, dn(zl, j)), dev(x=up(x, d)))

    def af(j):
        d = way(j)
        a_x[j, d].arrived()
        a_f[j].start(xa_at(dn(x, d), dn(zl, j)), xa_at(dn(x, d), dn(zl, j)), dev(x=up(x, d)))

    def share_a(d):
        b_a[d].arrived()
        a_s[d].start(ba_at(dn(y, d), c), ba_at(dn(y, d), c), dev(tok=sib))

    def project_a():
        for cp in own_a:
            cp.wait()
        all_of(a_x, a_f, b_a, a_s)
        for ys in range(NY):
            pa[ys] = jnp.dot(ba[...], xa[:, ys * quarter:(ys + 1) * quarter], preferred_element_type=F32)
        for d in THREE:
            p_a[d].start(pa.at[up(y, d)], ra.at[d - 1], dev(y=up(y, d)))

    def square_a():
        all_of(p_a)
        total = pa[y] + ra[0] + ra[1] + ra[2]
        sa[...] = (total * total).astype(BF16)
        for dt, dz in turns:
            t = up(tok, dt)
            s_z[dt, dz].start(sa.at[pl.ds(pl.multiple_of(t * da, da), da), :], sq_block(tok, x, zl, y),
                              dev(tok=t, zl=up(zl, dz)))
        own_s.append(local(sa.at[pl.ds(pl.multiple_of(tok * da, da), da), :], sq_block(tok, x, zl, y)))

    def spread(j):
        for d in SIDES:
            s_y[j, d].start(sq_chunk(dn(x, j), y), sq_chunk(dn(x, j), y), dev(y=up(y, d)))

    def spread_rest(j):
        for d in SIDES:
            u_x[j, d].start(sq_rest(x, dn(y, j)), sq_rest(x, dn(y, j)), dev(x=up(x, d)))

    def sx():
        own_s[0].wait()
        all_of(s_z)
        for d in SIDES:
            s_x[d].start(sq_chunk(x, y), sq_chunk(x, y), dev(x=up(x, d)))
        spread(0)
        for d in THREE:
            u_y[d].start(sq_rest(x, y), sq_rest(x, y), dev(y=up(y, d)))
        spread_rest(0)

    def sxf(i):
        d = SIDES[i]
        s_x[d].arrived()
        part = sq_chunk(dn(x, d), y, 128 * i, 128)
        s_xf[i].start(part, part, dev(x=up(x, d)))

    def ss(j):
        all_of(s_xf if j == 2 else [s_x[j]])
        spread(j)

    def sf(j):
        d = way(j)
        s_y[j, d].arrived()
        s_f[j].start(sq_chunk(dn(x, j), dn(y, d)), sq_chunk(dn(x, j), dn(y, d)), dev(y=up(y, d)))

    def us(j):
        u_y[j].arrived()
        spread_rest(j)

    def uf(j):
        d = way(j)
        u_x[j, d].arrived()
        u_f[j].start(sq_rest(dn(x, d), dn(y, j)), sq_rest(dn(x, d), dn(y, j)), dev(x=up(x, d)))

    def gz(d):
        g_z[d].start(main, xg_at(y, zl), dev(zl=up(zl, d)))

    def gs(j):
        g_z[j].arrived()
        for d in SIDES:
            g_y[j, d].start(xg_at(y, dn(zl, j)), xg_at(y, dn(zl, j)), dev(y=up(y, d)))

    def gf(j):
        d = way(j)
        g_y[j, d].arrived()
        g_f[j].start(xg_at(dn(y, d), dn(zl, j)), xg_at(dn(y, d), dn(zl, j)), dev(y=up(y, d)))

    def vz(i):
        if i:
            v_y[i].arrived()
        for d in THREE:
            v_z[i, d].start(xv_at(dn(y, i), zl) if i else rest, xv_at(dn(y, i), zl), dev(zl=up(zl, d)))

    def bx(h, k, d):
        b_x[h, k, d].start(bg_cols(h, mine[k], up(x, d)), bg_at(h, mine[k], x), dev(x=up(x, d)))

    def bs(h, k, d):
        b_x[h, k, d].arrived()
        b_s[h, k, d].start(bg_at(h, mine[k], dn(x, d)), bg_at(h, mine[k], dn(x, d)), dev(tok=sib))

    def cg(h, i):
        while own_g:
            own_g.pop().wait()
        for d in THREE:
            all_of([b_x[h, i // 2, d], b_s[h, i // 2, d]])
        ring = (0, 1, 3, 2)[i]
        if i == 0:
            all_of(g_z)
        elif i == 3:
            all_of(g_f)
        else:
            all_of([g_y[j, ring] for j in range(4)])
        all_of([v_z[ring, d] for d in THREE], [v_y[ring]] if ring else [])
        ys = dn(y, ring)
        rows = slice(NX * at[h], NX * (at[h] + PARTS[h]))
        part = jnp.dot(bg[ys, rows, :], xg[ys], preferred_element_type=F32)
        acc[rows, :] = part if i == 0 else acc[rows, :] + part
        if i == 3:
            ps[rows, :] = acc[rows, :].astype(BF16)
            for d in (2, 1, 3):
                xs = up(x, d)
                p_g[h, d].start(ps.at[part_rows(h, xs), :], pr.at[d - 1, rows_of(h), :], dev(x=xs))

    def square_g(h):
        all_of([p_g[h, d] for d in THREE])
        total = acc[part_rows(h, x), :]
        for d in range(NX - 1):
            total = total + pr[d, rows_of(h), :].astype(F32)
        sg[tok, rows_of(h), :] = (total * total).astype(BF16)
        t_far[h].start(sg_at(tok, h), sg_at(tok, h), dev(tok=far))
        t_sib[h].start(sg_at(tok, h), sg_at(tok, h), dev(tok=sib))

    def tb(h):
        t_far[h].arrived()
        t_both[h].start(sg_at(far, h), sg_at(far, h), dev(tok=sib))

    tile = 256
    scale = 1.0 / (cols * NT)

    def settle(recent):
        for tag, cp in [one for one in sent if one[0] not in recent]:
            cp.wait_send()
            sent.remove((tag, cp))

    def fin(i):
        if i == 0:
            settle(("s_y", "s_f", "u_x", "u_f", "t_far", "t_sib", "t_both"))
        all_of(*((s_x, s_xf, s_y, s_f, u_y, u_x, u_f), (t_sib,), (t_far,), (t_both,))[i])
        t = (tok, sib, far, up(sib, 2))[i]
        for n in range(0, out.shape[1], tile):
            part = lax.dot_general(sg[t], sq[t, n:n + tile, :], (((1,), (1,)), ((), ())), preferred_element_type=F32)
            value = part if i == 0 else out[:, n:n + tile] + part
            out[:, n:n + tile] = value * scale if i == 3 else value

    steps = {"ax": ax, "af": af, "as": share_a, "pa": project_a, "sa": square_a, "sx": sx, "sxf": sxf, "ss": ss, "sf": sf,
             "us": us, "uf": uf, "gz": gz, "gs": gs, "gf": gf, "vz": vz, "bx": bx, "bs": bs, "cg": cg, "sq": square_g, "tb": tb,
             "fin": fin}
    for name, *where in SCHEDULE:
        steps[name](*where)

    settle(())


def body(acts_t, grads_t, basis_a, basis_g):
    da, cols = acts_t.shape
    dg = grads_t.shape[0]
    fa = basis_a.shape[1] // NY
    rows_a, quarter = NY * da, cols // NY
    fx = NZ * dg
    anywhere = pl.BlockSpec(memory_space=pl.ANY)
    n_out = basis_a.shape[1] // NT
    return pl.pallas_call(
        kernel,
        out_shape=jax.ShapeDtypeStruct((dg, n_out), F32),
        in_specs=[anywhere] * 4,
        out_specs=pl.BlockSpec(memory_space=pltpu.VMEM),
        scratch_shapes=[
            pltpu.VMEM((fa, cols), BF16),
            pltpu.VMEM((rows_a, fa), BF16),
            pltpu.VMEM((NY, rows_a, quarter), F32),
            pltpu.VMEM((NY - 1, rows_a, quarter), F32),
            pltpu.VMEM((rows_a, quarter), BF16),
            pltpu.VMEM((NT, n_out, cols), BF16),
            pltpu.VMEM((NY, fx, cols), BF16),
            pltpu.VMEM((NY, NX * dg, fx), BF16),
            pltpu.VMEM((NX * dg, cols), F32),
            pltpu.VMEM((NX * dg, cols), BF16),
            pltpu.VMEM((NX - 1, dg, cols), BF16),
            pltpu.VMEM((NT, dg, cols), BF16),
            pltpu.SemaphoreType.DMA((N_COPIES,)),
            pltpu.SemaphoreType.DMA((N_COPIES,)),
            pltpu.SemaphoreType.DMA((N_LOCAL,)),
        ],
        compiler_params=pltpu.CompilerParams(
            collective_id=0, has_side_effects=True, vmem_limit_bytes=60 * 2**20
        ),
    )(acts_t, grads_t, basis_a, basis_g)


def solution(mesh):
    return jax.shard_map(
        body,
        mesh=mesh,
        in_specs=(P("col", "tok"), P("col", "tok"), P("col", None), P("col", None)),
        out_specs=P("col", "tok"),
        check_vma=False,
    )
```
